256 devices in a mesh: fsdp: 64 (over x, z, core), dp: 4 (over y).
Axes of the slice: x: 4, y: 4, z: 8, core: 2. Of those that a mesh axis runs over, the one named last changes fastest.
Arguments:
- grad_parts: bfloat16 [4, 48, 1024, 1024], P('dp', None, 'fsdp')
- block_owner: int32 [48], replicated, may hold values from 0 to 63, as said below
- left_stat: float32 [64, 1024, 1024], P('fsdp', 'dp')
- right_stat: float32 [64, 1024, 1024], P('fsdp', 'dp')
- root_left: float32 [64, 1024, 1024], P('fsdp', 'dp'), as said below
- root_right: float32 [64, 1024, 1024], P('fsdp', 'dp'), as said below
Outputs:
- left_updated: float32 [64, 1024, 1024], P('fsdp', 'dp')
- right_updated: float32 [64, 1024, 1024], P('fsdp', 'dp')
- direction: float32 [48, 1024, 1024], P(None, 'fsdp', 'dp')
The draws below stay inside these ranges and needn't reach their ends.
Inputs may be any that keep to these rules, and one draw needn't show every extreme that they name: `block_owner`: no two blocks share an owner; owners 0 and 63 always own a block. `root_right`: each slot is symmetric. `root_left`: each slot is symmetric.
All inputs are finite; a program needn't handle non-finite values.
Results may differ from the reference program's by a relative error of at most 0.0003.
Values may be sent and summed in bfloat16 or wider, within the bound.
No kernel may reach another device: no remote copies, remote signals or barrier semaphores. Data moves between devices by JAX's collectives and lax.ppermute only.
A program may use at most 64 MiB of HBM per device.

```python
import math
import jax
import jax.numpy as jnp
from jax import lax

B = 1024
NBLK = 48
N_FSDP = 64
N_DP = 4


def symmetric_draw(key, lowest, highest, spread):
    diag_key, off_key = jax.random.split(key, 2)
    normal_part = jax.random.normal(off_key, (N_FSDP, B, B), jnp.float32)
    rough = normal_part * (spread / math.sqrt(B))
    mirror = (rough + jnp.swapaxes(rough, 1, 2)) * 0.5
    diagonal = jnp.exp(jax.random.uniform(diag_key, (N_FSDP, B), jnp.float32, math.log(lowest), math.log(highest)))
    identity = jnp.eye(B, dtype=jnp.float32)
    return mirror * (1.0 - identity) + diagonal[:, :, None] * identity


def draw_left_stat(key, part):
    key = jax.random.fold_in(key, 11)
    return symmetric_draw(key, 0.5, 5.0, 0.7)


def draw_right_stat(key, part):
    key = jax.random.fold_in(key, 12)
    return symmetric_draw(key, 0.5, 5.0, 0.7)


def draw_root_left(key, part):
    key = jax.random.fold_in(key, 13)
    return symmetric_draw(key, 1.0, 4.0, 0.7)


def draw_root_right(key, part):
    key = jax.random.fold_in(key, 14)
    return symmetric_draw(key, 1.0, 4.0, 0.7)


def draw_grad_parts(key, part):
    key = jax.random.fold_in(key, 15)
    row_key, col_key, own_key = jax.random.split(key, 3)
    own = jnp.clip(jax.random.normal(own_key, (N_DP, NBLK, B, B), jnp.float32), -4.0, 4.0)
    row_scale = jnp.exp(jax.random.uniform(row_key, (1, NBLK, B, 1), jnp.float32, math.log(0.3), math.log(3.0)))
    col_scale = jnp.exp(jax.random.uniform(col_key, (1, NBLK, 1, B), jnp.float32, math.log(0.3), math.log(3.0)))
    mixed = own
    return (mixed * row_scale * col_scale).astype(jnp.bfloat16)


def draw_block_owner(key, part):
    key = jax.random.fold_in(key, 16)
    first_key, second_key = jax.random.split(key)
    middle = jax.random.permutation(first_key, N_FSDP - 2) + 1
    ends = jnp.array([0, N_FSDP - 1], dtype=jnp.int32)
    chosen = jnp.concatenate([ends, middle[:NBLK - 2].astype(jnp.int32)]).astype(jnp.int32)
    return jax.random.permutation(second_key, chosen).astype(jnp.int32)


def setup_inputs(seed: int = 0) -> dict:
    key_list = jax.random.split(jax.random.key(seed), 7)
    grad_parts = draw_grad_parts(jax.random.fold_in(key_list[6], 71), 0)
    block_owner = draw_block_owner(jax.random.fold_in(key_list[6], 71), 0)
    left_stat = draw_left_stat(jax.random.fold_in(key_list[6], 71), 0)
    right_stat = draw_right_stat(jax.random.fold_in(key_list[6], 71), 0)
    root_left = draw_root_left(jax.random.fold_in(key_list[6], 71), 0)
    root_right = draw_root_right(jax.random.fold_in(key_list[6], 71), 0)
    return dict(grad_parts=grad_parts, block_owner=block_owner, left_stat=left_stat, right_stat=right_stat, root_left=root_left, root_right=root_right)


AVERAGING = 0.9
GRAFT_EPS = 1e-06

def reference(grad_parts, block_owner, left_stat, right_stat, root_left, root_right):
    precise = lax.Precision.HIGHEST
    summed = lax.optimization_barrier(jnp.sum(grad_parts.astype(jnp.float32), axis=0))
    owner_ids = jnp.arange(N_FSDP, dtype=jnp.int32)

    def one_owner(inputs):
        owner_id, left_one, right_one, left_root, right_root = inputs
        matches = (block_owner == owner_id).astype(jnp.int32)
        position = jnp.argmax(matches).astype(jnp.int32)
        present = jnp.sum(matches) > 0
        picked = lax.dynamic_index_in_dim(summed, position, 0, keepdims=False)
        gradient = jnp.where(present, picked, jnp.zeros_like(picked))
        left_new = AVERAGING * left_one + (1.0 - AVERAGING) * jnp.dot(gradient, gradient.T, precision=precise) / B
        right_new = AVERAGING * right_one + (1.0 - AVERAGING) * jnp.dot(gradient.T, gradient, precision=precise) / B
        partial_value = jnp.dot(left_root, gradient, precision=precise)
        precond = jnp.dot(partial_value, right_root, precision=precise)
        factor = jnp.sqrt(jnp.sum(gradient * gradient)) * lax.rsqrt(jnp.sum(precond * precond) + GRAFT_EPS)
        return (left_new, right_new, precond * factor)
    left_updated, right_updated, grafted = lax.map(one_owner, (owner_ids, left_stat, right_stat, root_left, root_right))
    direction = jnp.take(grafted, block_owner, axis=0)
    return (left_updated, right_updated, direction)
```

```python
import functools

import jax
import jax.numpy as jnp
from jax import lax
from jax.experimental import pallas as pl
from jax.experimental.pallas import tpu as pltpu
from jax.sharding import PartitionSpec as P

AVERAGING = 0.9
GRAFT_EPS = 1e-06
VMEM_LIMIT = 48 * 1024 * 1024

VMEM = pl.BlockSpec(memory_space=pltpu.VMEM)
SMEM = pl.BlockSpec(memory_space=pltpu.SMEM)


def split(value):
    high = value.astype(jnp.bfloat16)
    low = (value - high.astype(jnp.float32)).astype(jnp.bfloat16)
    return high, low


def dot3(left, right, left_dim, right_dim):
    dims = (((left_dim,), (right_dim,)), ((), ()))

    def one(a, b):
        return lax.dot_general(a, b, dims, preferred_element_type=jnp.float32)

    return one(left[0], right[0]) + (one(left[0], right[1]) + one(left[1], right[0]))


def call(kernel, out_shape, in_specs, out_specs, flops, bytes_accessed, **kwargs):
    return pl.pallas_call(
        kernel,
        out_shape=out_shape,
        in_specs=in_specs,
        out_specs=out_specs,
        compiler_params=pltpu.CompilerParams(vmem_limit_bytes=VMEM_LIMIT),
        cost_estimate=pl.CostEstimate(
            flops=flops, bytes_accessed=bytes_accessed, transcendentals=0
        ),
        **kwargs,
    )


def select_kernel(owner_ref, grad_ref, out_ref):
    blocks = grad_ref.shape[0]
    part = out_ref.shape[2]
    parts = grad_ref.shape[2] // part
    out_ref[...] = jnp.zeros_like(out_ref)

    @pl.loop(0, blocks)
    def _(b):
        first = owner_ref[b] * parts
        for d in range(parts):
            out_ref[first + d] = grad_ref[b, :, d * part : (d + 1) * part]


def sum_kernel(arrived_ref, out_ref, square_ref):
    slabs, replicas, rows, part = arrived_ref.shape
    total = arrived_ref[:, 0].astype(jnp.float32)
    for r in range(1, replicas):
        total = total + arrived_ref[:, r].astype(jnp.float32)
    total = total.reshape(slabs * rows, part)
    high, low = split(total)
    out_ref[:, :part] = high
    out_ref[:, part:] = low
    square_ref[0, 0] = jnp.sum(total * total)


def halves(ref, part, rows=None):
    if rows is None:
        return ref[:, :part], ref[:, part:]
    return ref[rows, :part], ref[rows, part:]


def step_kernel(
    scale, sources, first, place_ref, own_ref, *refs
):
    parts, refs = refs[: len(sources)], refs[len(sources) :]
    root_ref, left_in, right_in = refs[:3]
    refs = refs[3:]
    if not first:
        value_in, refs = refs[0], refs[1:]
    left_out, right_out, value_out = refs
    part = own_ref.shape[1] // 2
    me = place_ref[0]
    my_rows = pl.ds(pl.multiple_of(me * part, part), part)
    own = halves(own_ref, part)
    left = left_in[...]
    if first:
        left = left * AVERAGING
        right_out[...] = right_in[...] * AVERAGING
    else:
        right_out[...] = right_in[...]
    value = None if first else value_in[...]
    for shift, ref in zip(sources, parts):
        source = lax.rem(me + shift, 4)
        columns = pl.ds(pl.multiple_of(source * part, part), part)
        block = halves(ref, part)
        left = left + scale * dot3(halves(ref, part, my_rows), block, 1, 1)
        right_out[:, columns] += scale * dot3(own, block, 0, 0)
        term = dot3(block, split(root_ref[:, columns]), 1, 1)
        value = term if value is None else value + term
    left_out[...] = left
    value_out[...] = value


def step(scale, sources, place, own, parts, root, left, right, value):
    first = value is None
    part, order = left.shape
    operands = [place, own, *parts, root, left, right] + ([] if first else [value])
    specs = [SMEM] + [VMEM] * (len(operands) - 1)
    f32 = jnp.float32
    return call(
        functools.partial(step_kernel, scale, sources, first),
        (
            jax.ShapeDtypeStruct((part, order), f32),
            jax.ShapeDtypeStruct((part, order), f32),
            jax.ShapeDtypeStruct((order, part), f32),
        ),
        specs,
        (VMEM, VMEM, VMEM),
        len(sources) * 3 * 3 * 2 * part * part * order,
        (6 + len(sources)) * part * order * 4,
    )(*operands)


def precondition_kernel(root_ref, value_ref, out_ref, square_ref):
    rows = value_ref.shape[1]
    value = split(value_ref[...])
    total = jnp.zeros((), jnp.float32)
    for i in range(root_ref.shape[0] // rows):
        block = dot3(split(root_ref[i * rows : (i + 1) * rows, :]), value, 1, 0)
        out_ref[i * rows : (i + 1) * rows, :] = block
        total = total + jnp.sum(block * block)
    square_ref[0, 0] = total


def reorder_kernel(owner_ref, factor_ref, returned_ref, out_ref):
    @pl.loop(0, out_ref.shape[0])
    def _(b):
        owner = owner_ref[b]
        out_ref[b] = returned_ref[owner] * factor_ref[owner]


def per_device(grad_parts, block_owner, left_stat, right_stat, root_left, root_right):
    owners = lax.axis_size("fsdp")
    replicas = lax.axis_size("dp")
    me = lax.axis_index("dp")
    part, order = root_left.shape[1:]
    blocks, slab = grad_parts.shape[1:3]
    f32, bf16 = jnp.float32, jnp.bfloat16
    scale = (1.0 - AVERAGING) / order
    place = me.astype(jnp.int32).reshape(1)
    scalar = jax.ShapeDtypeStruct((1, 1), f32)
    around = [(i, (i + 1) % replicas) for i in range(replicas)]
    back = [(i, (i - 1) % replicas) for i in range(replicas)]

    whole_root = lax.all_gather(root_left[0], "dp", axis=0, tiled=True)
    outgoing = call(
        select_kernel,
        jax.ShapeDtypeStruct((owners * replicas, slab, part), bf16),
        [SMEM, VMEM],
        VMEM,
        0,
        4 * blocks * slab * order,
    )(block_owner, grad_parts[0])
    arrived = lax.all_to_all(outgoing, ("fsdp", "dp"), split_axis=0, concat_axis=0, tiled=True)
    own, own_square = call(
        sum_kernel,
        (jax.ShapeDtypeStruct((order, 2 * part), bf16), scalar),
        [VMEM],
        (VMEM, SMEM),
        0,
        12 * order * part,
    )(arrived.reshape(owners, replicas, slab, part))

    before = lax.ppermute(own, "dp", around)
    after = lax.ppermute(own, "dp", back)
    half = order // 2
    far = jnp.concatenate(
        [lax.ppermute(before[:half], "dp", around), lax.ppermute(after[half:], "dp", back)], axis=0
    )
    root = root_right[0]
    left, right, value = step(
        scale, (0,), place, own, (own,), root, left_stat[0], right_stat[0], None
    )
    left, right, value = step(
        scale, (3, 1), place, own, (before, after), root, left, right, value
    )
    left, right, value = step(scale, (2,), place, own, (far,), root, left, right, value)
    result, square = call(
        precondition_kernel,
        (jax.ShapeDtypeStruct((order, part), f32), scalar),
        [VMEM, VMEM],
        (VMEM, SMEM),
        6 * order * order * part,
        4 * order * (order + 2 * part),
    )(whole_root, value)

    squares = jnp.concatenate([own_square, square], axis=1)
    squares = lax.all_gather(squares, ("fsdp", "dp"), axis=0, tiled=True)
    squares = jnp.sum(squares.reshape(owners, replicas, 2), axis=1)
    factor = jnp.sqrt(squares[:, 0]) * lax.rsqrt(squares[:, 1] + GRAFT_EPS)
    returned = lax.all_to_all(
        result.reshape(owners, slab, part), "fsdp", split_axis=0, concat_axis=0, tiled=True
    )
    direction = call(
        reorder_kernel,
        jax.ShapeDtypeStruct((blocks, slab, part), f32),
        [SMEM, SMEM, VMEM],
        VMEM,
        0,
        8 * blocks * slab * part,
    )(block_owner, factor, returned)
    return (left[None], right[None], direction)


def solution(mesh):
    placed = (
        P("dp", None, "fsdp", None),
        P(),
        P("fsdp", "dp", None),
        P("fsdp", "dp", None),
        P("fsdp", "dp", None),
        P("fsdp", "dp", None),
    )
    return jax.shard_map(
        per_device,
        mesh=mesh,
        in_specs=placed,
        out_specs=(P("fsdp", "dp", None), P("fsdp", "dp", None), P(None, "fsdp", "dp")),
        check_vma=False,
    )
```

```python
import functools

import jax
import jax.numpy as jnp
from jax import lax
from jax.experimental import pallas as pl
from jax.experimental.pallas import tpu as pltpu
from jax.sharding import PartitionSpec as P

AVERAGING = 0.9
GRAFT_EPS = 1e-06
VMEM_LIMIT = 24 * 1024 * 1024

VMEM = pl.BlockSpec(memory_space=pltpu.VMEM)
SMEM = pl.BlockSpec(memory_space=pltpu.SMEM)
F32, BF16 = jnp.float32, jnp.bfloat16


def split(value):
    high = value.astype(BF16)
    low = (value - high.astype(F32)).astype(BF16)
    return high, low


def dot3(left, right, left_dim, right_dim):
    dims = (((left_dim,), (right_dim,)), ((), ()))

    def one(a, b):
        return lax.dot_general(a, b, dims, preferred_element_type=F32)

    return one(left[0], right[0]) + (one(left[0], right[1]) + one(left[1], right[0]))


def like(shape, dtype=F32):
    return jax.ShapeDtypeStruct(shape, dtype)


def call(kernel, outs, operands, n_smem=0, smem_outs=(), flops=0, cost=4 << 20):
    several = isinstance(outs, tuple)
    out_specs = tuple(
        SMEM if i in smem_outs else VMEM for i in range(len(outs) if several else 1)
    )
    return pl.pallas_call(
        kernel,
        out_shape=outs,
        in_specs=[SMEM] * n_smem + [VMEM] * (len(operands) - n_smem),
        out_specs=out_specs if several else out_specs[0],
        compiler_params=pltpu.CompilerParams(vmem_limit_bytes=VMEM_LIMIT),
        cost_estimate=pl.CostEstimate(flops=flops, bytes_accessed=cost, transcendentals=0),
    )(*operands)


def around(index, size, parts):
    return pl.ds(pl.multiple_of(lax.rem(index, parts) * size, size), size)


def pack_kernel(place_ref, grad_ref, *out_refs):
    part = out_refs[0].shape[2]
    parts = len(out_refs)
    for k, out_ref in enumerate(out_refs):
        out_ref[...] = grad_ref[:, :, around(place_ref[0] + k, part, parts)]


def sum_kernel(owner_ref, *refs):
    *replica_refs, out_ref = refs
    part = out_ref.shape[2] // 2
    out_ref[...] = jnp.zeros_like(out_ref)

    @pl.loop(0, replica_refs[0].shape[0])
    def _(b):
        total = replica_refs[0][b].astype(F32)
        for ref in replica_refs[1:]:
            total = total + ref[b].astype(F32)
        high, low = split(total)
        owner = owner_ref[b]
        out_ref[owner, :, :part] = high
        out_ref[owner, :, part:] = low


def root_pack_kernel(place_ref, root_ref, next_ref, previous_ref, far_ref):
    size = root_ref.shape[0]
    parts = root_ref.shape[1] // size
    me = place_ref[0]

    def put(ref, slot, shift):
        high, low = split(root_ref[:, around(me + shift, size, parts)])
        ref[0, :, slot * size : (slot + 1) * size] = high
        ref[1, :, slot * size : (slot + 1) * size] = low

    for slot in range(3):
        put(next_ref, slot, slot)
    put(previous_ref, 0, 0)
    put(previous_ref, 1, parts - 1)
    put(far_ref, 0, 0)


def root_join_kernel(place_ref, root_ref, after_ref, before_ref, far_ref, high_ref, low_ref):
    size = root_ref.shape[0]
    parts = root_ref.shape[1] // size
    me = place_ref[0]

    def put(i, j, value):
        rows, columns = around(me + i, size, parts), around(me + j, size, parts)
        for ref, half in zip((high_ref, low_ref), value):
            ref[rows, columns] = half
            if i != j:
                ref[columns, rows] = half.astype(F32).T.astype(BF16)

    def block(ref, slot):
        columns = slice(slot * size, (slot + 1) * size)
        return ref[0, :, columns], ref[1, :, columns]

    for j in range(parts):
        put(0, j, split(root_ref[:, around(me + j, size, parts)]))
    put(1, 1, block(after_ref, 0))
    put(1, 2, block(after_ref, 1))
    put(1, 3, block(after_ref, 2))
    put(3, 3, block(before_ref, 0))
    put(3, 2, block(before_ref, 1))
    put(2, 2, block(far_ref, 0))


def own_half(refs, me, part):
    rows = pl.ds(pl.multiple_of(lax.rem(me, 2) * part, part), part)
    top, bottom = refs[0][rows, :], refs[1][rows, :]
    return jnp.where(me < 2, top, bottom)


def pair(value):
    part = value.shape[1] // 2
    return value[:, :part], value[:, part:]


def statistics_kernel(scale, shifts, first, place_ref, *refs):
    count = 2 * len(shifts)
    own, parts = refs[:2], refs[2 : 2 + count]
    left_in, right_in, left_out, right_out = refs[2 + count :]
    me = place_ref[0]
    part, order = left_in.shape
    half = order // 2
    keep = AVERAGING if first else 1.0
    right_out[...] = right_in[...] * keep
    left = left_in[...] * keep
    sums = [left[:, :half], left[:, half:]]
    for i, shift in enumerate(shifts):
        blocks = parts[2 * i : 2 * i + 2]
        mine = pair(own_half(blocks, me, part))
        halves = [pair(ref[...]) for ref in blocks]
        for h in range(2):
            sums[h] = sums[h] + scale * dot3(mine, halves[h], 1, 1)
        term = dot3(pair(own[0][...]), halves[0], 0, 0) + dot3(pair(own[1][...]), halves[1], 0, 0)
        columns = around(me + shift, part, order // part)
        right_out[:, columns] += scale * term
    left_out[:, :half] = sums[0]
    left_out[:, half:] = sums[1]


def value_terms(me, shifts, parts, root_ref):
    part, order = root_ref.shape
    sums = [None, None]
    for i, shift in enumerate(shifts):
        root = split(root_ref[:, around(me + shift, part, order // part)])
        for h in range(2):
            term = dot3(pair(parts[2 * i + h][...]), root, 1, 1)
            sums[h] = term if sums[h] is None else sums[h] + term
    return sums


def value_kernel(shifts, first, place_ref, *refs):
    count = 2 * len(shifts)
    parts, root_ref = refs[:count], refs[count]
    *value_in, value_out = refs[count + 1 :]
    half = value_out.shape[0] // 2
    sums = value_terms(place_ref[0], shifts, parts, root_ref)
    for h in range(2):
        rows = slice(h * half, (h + 1) * half)
        value_out[rows, :] = sums[h] if first else sums[h] + value_in[0][rows, :]


def result_kernel(shift, place_ref, top_ref, bottom_ref, root_ref, value_ref, high_ref, low_ref, own_top, own_bottom, out_ref, square_ref):
    order, part = value_ref.shape
    half = order // 2
    sums = value_terms(place_ref[0], (shift,), (top_ref, bottom_ref), root_ref)
    halves = [split(sums[h] + value_ref[h * half : (h + 1) * half, :]) for h in range(2)]
    value = [jnp.concatenate([halves[0][i], halves[1][i]], axis=0) for i in range(2)]
    total = jnp.zeros((), F32)
    for i in range(order // part):
        rows = slice(i * part, (i + 1) * part)
        block = dot3((high_ref[rows, :], low_ref[rows, :]), value, 1, 0)
        out_ref[rows, :] = block
        total = total + jnp.sum(block * block)
    gradient = jnp.zeros((), F32)
    for ref in (own_top, own_bottom):
        high, low = pair(ref[...])
        whole = high.astype(F32) + low.astype(F32)
        gradient = gradient + jnp.sum(whole * whole)
    first = lax.broadcasted_iota(jnp.int32, square_ref.shape, 1) == 0
    square_ref[...] = jnp.where(first, gradient, total)


def scale_kernel(factor_ref, value_ref, out_ref):
    out_ref[...] = value_ref[...] * factor_ref[0, 0]


def reorder_kernel(owner_ref, returned_ref, out_ref):
    @pl.loop(0, out_ref.shape[0])
    def _(b):
        out_ref[b] = returned_ref[owner_ref[b]]


def per_device(grad_parts, block_owner, left_stat, right_stat, root_left, root_right):
    owners = lax.axis_size("fsdp")
    replicas = lax.axis_size("dp")
    me = lax.axis_index("dp")
    part, order = root_left.shape[1:]
    blocks, slab = grad_parts.shape[1:3]
    scale = (1.0 - AVERAGING) / order
    place = me.astype(jnp.int32).reshape(1)
    half = order // 2
    macs = 2 * 3 * part * part * order

    def shifted(value, k):
        return lax.ppermute(value, "dp", [(i, (i + k) % replicas) for i in range(replicas)])

    packed = call(
        pack_kernel, (like((blocks, slab, part), BF16),) * replicas, [place, grad_parts[0]], 1
    )
    arrived = [packed[0]] + [shifted(packed[k], k) for k in (1, 3, 2)]
    to_previous, to_next, to_far = call(
        root_pack_kernel,
        (like((2, part, 3 * part), BF16), like((2, part, 2 * part), BF16), like((2, part, part), BF16)),
        [place, root_left[0]],
        1,
    )
    arrived, to_previous, to_next, to_far = lax.optimization_barrier(
        (arrived, to_previous, to_next, to_far)
    )
    root_after = shifted(to_previous, 3)
    root_before = shifted(to_next, 1)
    root_far = shifted(to_far, 2)
    outgoing = call(
        sum_kernel, like((owners, slab, 2 * part), BF16), [block_owner, *arrived], 1
    )
    own = lax.all_to_all(outgoing, "fsdp", split_axis=0, concat_axis=0, tiled=True)
    own = own.reshape(order, 2 * part)
    own, root_after, root_before, root_far = lax.optimization_barrier(
        (own, root_after, root_before, root_far)
    )
    own = (own[:half], own[half:])

    before_top = shifted(own[0], 1)
    after_bottom = shifted(own[1], 3)
    before_bottom = shifted(own[1], 1)
    after_top = shifted(own[0], 3)
    far_top = shifted(before_top, 1)
    far_bottom = shifted(after_bottom, 3)

    root = root_right[0]
    stat = like((part, order))
    left, right = call(
        functools.partial(statistics_kernel, scale, (0,), True),
        (stat, stat),
        [place, *own, *own, left_stat[0], right_stat[0]],
        1,
        flops=2 * macs,
    )
    value = call(
        functools.partial(value_kernel, (0,), True),
        like((order, part)),
        [place, *own, root],
        1,
        flops=macs,
    )
    high, low = call(
        root_join_kernel,
        (like((order, order), BF16),) * 2,
        [place, root_left[0], root_after, root_before, root_far],
        1,
        cost=16 << 20,
    )
    near = (before_top, before_bottom, after_top, after_bottom)
    left, right = call(
        functools.partial(statistics_kernel, scale, (3, 1), False),
        (stat, stat),
        [place, *own, *near, left, right],
        1,
        flops=4 * macs,
    )
    value = call(
        functools.partial(value_kernel, (3, 1), False),
        like((order, part)),
        [place, *near, root, value],
        1,
        flops=2 * macs,
    )
    result, square = call(
        functools.partial(result_kernel, 2),
        (like((order, part)), like((8, 128))),
        [place, far_top, far_bottom, root, value, high, low, *own],
        1,
        flops=5 * macs,
    )
    squares = square + shifted(square, 1) + shifted(square, 3) + shifted(square, 2)
    left, right = call(
        functools.partial(statistics_kernel, scale, (2,), False),
        (stat, stat),
        [place, *own, far_top, far_bottom, left, right],
        1,
        flops=2 * macs,
    )
    factor = jnp.sqrt(squares[:1, :1]) * lax.rsqrt(squares[:1, 1:2] + GRAFT_EPS)
    grafted = call(scale_kernel, like((order, part)), [factor, result], 1)
    returned = lax.all_to_all(
        grafted.reshape(owners, slab, part), "fsdp", split_axis=0, concat_axis=0, tiled=True
    )
    direction = call(
        reorder_kernel, like((blocks, slab, part)), [block_owner, returned], 1
    )
    return (left[None], right[None], direction)


def solution(mesh):
    placed = (
        P("dp", None, "fsdp", None),
        P(),
        P("fsdp", "dp", None),
        P("fsdp", "dp", None),
        P("fsdp", "dp", None),
        P("fsdp", "dp", None),
    )
    return jax.shard_map(
        per_device,
        mesh=mesh,
        in_specs=placed,
        out_specs=(P("fsdp", "dp", None), P("fsdp", "dp", None), P(None, "fsdp", "dp")),
        check_vma=False,
    )
```

```python
import functools
import math

import jax
import jax.numpy as jnp
from jax import lax
from jax.experimental import pallas as pl
from jax.experimental.pallas import tpu as pltpu
from jax.sharding import PartitionSpec as P

AVERAGING = 0.9
GRAFT_EPS = 1e-06
VMEM_LIMIT = 24 * 1024 * 1024
STEPS = 1344
LARGEST = 252 * 128 + 127

VMEM = pl.BlockSpec(memory_space=pltpu.VMEM)
SMEM = pl.BlockSpec(memory_space=pltpu.SMEM)
F32, BF16 = jnp.float32, jnp.bfloat16


def split(value):
    high = value.astype(BF16)
    low = (value - high.astype(F32)).astype(BF16)
    return high, low


def dot3(left, right, left_dim, right_dim):
    dims = (((left_dim,), (right_dim,)), ((), ()))

    def one(a, b):
        return lax.dot_general(a, b, dims, preferred_element_type=F32)

    return one(left[0], right[0]) + (one(left[0], right[1]) + one(left[1], right[0]))


def like(shape, dtype=F32):
    return jax.ShapeDtypeStruct(shape, dtype)


def call(kernel, outs, operands, n_smem=0, smem_outs=(), flops=0, cost=4 << 20):
    several = isinstance(outs, tuple)
    out_specs = tuple(
        SMEM if i in smem_outs else VMEM for i in range(len(outs) if several else 1)
    )
    return pl.pallas_call(
        kernel,
        out_shape=outs,
        in_specs=[SMEM] * n_smem + [VMEM] * (len(operands) - n_smem),
        out_specs=out_specs if several else out_specs[0],
        compiler_params=pltpu.CompilerParams(vmem_limit_bytes=VMEM_LIMIT),
        cost_estimate=pl.CostEstimate(flops=flops, bytes_accessed=cost, transcendentals=0),
    )(*operands)


def around(index, size, parts):
    return pl.ds(pl.multiple_of(lax.rem(index, parts) * size, size), size)


def pack_kernel(place_ref, grad_ref, *out_refs):
    part = out_refs[0].shape[2]
    parts = len(out_refs)
    for k, out_ref in enumerate(out_refs):
        out_ref[...] = grad_ref[:, :, around(place_ref[0] + k, part, parts)]


def sum_kernel(owner_ref, *refs):
    *replica_refs, out_ref = refs
    part = out_ref.shape[2] // 2
    out_ref[...] = jnp.zeros_like(out_ref)

    @pl.loop(0, replica_refs[0].shape[0])
    def _(b):
        total = replica_refs[0][b].astype(F32)
        for ref in replica_refs[1:]:
            total = total + ref[b].astype(F32)
        high, low = split(total)
        owner = owner_ref[b]
        out_ref[owner, :, :part] = high
        out_ref[owner, :, part:] = low


def root_pack_kernel(place_ref, root_ref, next_ref, previous_ref, far_ref):
    size = root_ref.shape[0]
    parts = root_ref.shape[1] // size
    me = place_ref[0]

    def put(ref, slot, shift):
        high, low = split(root_ref[:, around(me + shift, size, parts)])
        ref[0, :, slot * size : (slot + 1) * size] = high
        ref[1, :, slot * size : (slot + 1) * size] = low

    for slot in range(3):
        put(next_ref, slot, slot)
    put(previous_ref, 0, 0)
    put(previous_ref, 1, parts - 1)
    put(far_ref, 0, 0)


def root_join_kernel(place_ref, root_ref, after_ref, before_ref, far_ref, high_ref, low_ref):
    size = root_ref.shape[0]
    parts = root_ref.shape[1] // size
    me = place_ref[0]

    def put(i, j, value):
        rows, columns = around(me + i, size, parts), around(me + j, size, parts)
        for ref, half in zip((high_ref, low_ref), value):
            ref[rows, columns] = half
            if i != j:
                ref[columns, rows] = half.astype(F32).T.astype(BF16)

    def block(ref, slot):
        columns = slice(slot * size, (slot + 1) * size)
        return ref[0, :, columns], ref[1, :, columns]

    for j in range(parts):
        put(0, j, split(root_ref[:, around(me + j, size, parts)]))
    put(1, 1, block(after_ref, 0))
    put(1, 2, block(after_ref, 1))
    put(1, 3, block(after_ref, 2))
    put(3, 3, block(before_ref, 0))
    put(3, 2, block(before_ref, 1))
    put(2, 2, block(far_ref, 0))


def own_half(refs, me, part):
    rows = pl.ds(pl.multiple_of(lax.rem(me, 2) * part, part), part)
    top, bottom = refs[0][rows, :], refs[1][rows, :]
    return jnp.where(me < 2, top, bottom)


def pair(value):
    part = value.shape[1] // 2
    return value[:, :part], value[:, part:]


def statistics_kernel(scale, shifts, first, place_ref, *refs):
    count = 2 * len(shifts)
    own, parts = refs[:2], refs[2 : 2 + count]
    left_in, right_in, left_out, right_out = refs[2 + count :]
    me = place_ref[0]
    part, order = left_in.shape
    half = order // 2
    keep = AVERAGING if first else 1.0
    right_out[...] = right_in[...] * keep
    left = left_in[...] * keep
    sums = [left[:, :half], left[:, half:]]
    for i, shift in enumerate(shifts):
        blocks = parts[2 * i : 2 * i + 2]
        mine = pair(own_half(blocks, me, part))
        halves = [pair(ref[...]) for ref in blocks]
        for h in range(2):
            sums[h] = sums[h] + scale * dot3(mine, halves[h], 1, 1)
        term = dot3(pair(own[0][...]), halves[0], 0, 0) + dot3(pair(own[1][...]), halves[1], 0, 0)
        columns = around(me + shift, part, order // part)
        right_out[:, columns] += scale * term
    left_out[:, :half] = sums[0]
    left_out[:, half:] = sums[1]


def value_terms(me, shifts, parts, root_ref):
    part, order = root_ref.shape
    sums = [None, None]
    for i, shift in enumerate(shifts):
        root = split(root_ref[:, around(me + shift, part, order // part)])
        for h in range(2):
            term = dot3(pair(parts[2 * i + h][...]), root, 1, 1)
            sums[h] = term if sums[h] is None else sums[h] + term
    return sums


def value_kernel(shifts, first, place_ref, *refs):
    count = 2 * len(shifts)
    parts, root_ref = refs[:count], refs[count]
    *value_in, value_out = refs[count + 1 :]
    half = value_out.shape[0] // 2
    sums = value_terms(place_ref[0], shifts, parts, root_ref)
    for h in range(2):
        rows = slice(h * half, (h + 1) * half)
        value_out[rows, :] = sums[h] if first else sums[h] + value_in[0][rows, :]


def square_kernel(top_ref, bottom_ref, out_ref):
    total = jnp.zeros((), F32)
    for ref in (top_ref, bottom_ref):
        high, low = pair(ref[...])
        whole = high.astype(F32) + low.astype(F32)
        total = total + jnp.sum(whole * whole)
    out_ref[...] = jnp.full(out_ref.shape, total)


def result_kernel(
    shift, place_ref, top_ref, bottom_ref, root_ref, value_ref, high_ref, low_ref, own_square, out_ref, square_ref, peak_ref
):
    order, part = value_ref.shape
    half = order // 2
    sums = value_terms(place_ref[0], (shift,), (top_ref, bottom_ref), root_ref)
    halves = [split(sums[h] + value_ref[h * half : (h + 1) * half, :]) for h in range(2)]
    value = [jnp.concatenate([halves[0][i], halves[1][i]], axis=0) for i in range(2)]
    total = jnp.zeros((), F32)
    peak = jnp.zeros((), F32)
    for i in range(order // part):
        rows = slice(i * part, (i + 1) * part)
        block = dot3((high_ref[rows, :], low_ref[rows, :]), value, 1, 0)
        out_ref[rows, :] = block
        total = total + jnp.sum(block * block)
        peak = jnp.maximum(peak, jnp.max(jnp.abs(block)))
    first = lax.broadcasted_iota(jnp.int32, square_ref.shape, 1) == 0
    square_ref[...] = jnp.where(first, own_square[...], total)
    peak_ref[...] = jnp.full(peak_ref.shape, peak)


def encode(ratio):
    size = jnp.abs(ratio)
    code = jnp.floor(jnp.log(jnp.maximum(size, 1e-30)) * (STEPS / math.log(2.0)) + (LARGEST + 0.5))
    code = jnp.minimum(code, float(LARGEST))
    exponent = jnp.floor(code * (1.0 / 128.0))
    root = jnp.exp2((exponent - 126.0) * 0.5)
    number = (1.0 + (code - exponent * 128.0) * (1.0 / 128.0)) * root * root
    number = jnp.where(code < 128.0, 0.0, number)
    return jnp.where(ratio < 0.0, -number, number).astype(BF16)


def decode(number):
    number = number.astype(F32)
    size = jnp.abs(number)
    exponent = jnp.floor(jnp.log(jnp.maximum(size, 1e-38)) * (1.0 / math.log(2.0)) + 0.002)
    root = jnp.exp2(exponent * -0.5)
    code = 128.0 * (exponent + 125.0 + size * root * root)
    value = jnp.exp2((code - LARGEST) * (1.0 / STEPS))
    value = jnp.where(size == 0.0, 0.0, value)
    return jnp.where(number < 0.0, -value, value)


def encode_kernel(value_ref, peak_ref, out_ref):
    slab = value_ref.shape[0] // out_ref.shape[0]
    lanes = out_ref.shape[2]
    peak = jnp.max(peak_ref[...])
    inverse = jnp.where(peak > 1e-37, 1.0 / jnp.maximum(peak, 1e-37), 0.0)
    pieces = value_ref.shape[1] // lanes

    @pl.loop(0, out_ref.shape[0], unroll=4)
    def _(o):
        rows = pl.ds(pl.multiple_of(o * slab, slab), slab)
        for i in range(pieces):
            value = value_ref[rows, i * lanes : (i + 1) * lanes]
            out_ref[o, i * slab : (i + 1) * slab, :] = encode(value * inverse)


def stamp_kernel(peak_ref, *refs):
    *square_refs, codes_ref, out_ref = refs
    total = square_refs[0][...]
    for ref in square_refs[1:]:
        total = total + ref[...]
    count, rows, lanes = out_ref.shape
    gradient, result = total[:, :1], total[:, 1:2]
    scale = peak_ref[...] * (jnp.sqrt(gradient) * lax.rsqrt(result + GRAFT_EPS))
    row = lax.broadcasted_iota(jnp.int32, scale.shape, 0)
    high = scale.astype(BF16).astype(F32)
    middle = (scale - high).astype(BF16).astype(F32)
    low = scale - high - middle
    value = jnp.where(row == 0, high, jnp.where(row == 1, middle, jnp.where(row == 2, low, 0.0)))
    tall = scale.shape[0]
    out_ref[:, : rows - tall, :] = codes_ref[...]
    out_ref[:, rows - tall :, :] = jnp.broadcast_to(value.astype(BF16)[None], (count, tall, lanes))


def reorder_kernel(owner_ref, returned_ref, out_ref):
    slab = out_ref.shape[1]
    rows, lanes = returned_ref.shape[1:]
    pieces = out_ref.shape[2] // lanes

    @pl.loop(0, out_ref.shape[0], unroll=4)
    def _(b):
        owner = owner_ref[b]
        scale = jnp.sum(returned_ref[owner, pieces * slab :, :].astype(F32), axis=0, keepdims=True)
        for i in range(pieces):
            value = decode(returned_ref[owner, i * slab : (i + 1) * slab, :])
            out_ref[b, :, i * lanes : (i + 1) * lanes] = value * scale


def per_device(grad_parts, block_owner, left_stat, right_stat, root_left, root_right):
    owners = lax.axis_size("fsdp")
    replicas = lax.axis_size("dp")
    me = lax.axis_index("dp")
    part, order = root_left.shape[1:]
    blocks, slab = grad_parts.shape[1:3]
    scale = (1.0 - AVERAGING) / order
    place = me.astype(jnp.int32).reshape(1)
    half = order // 2
    macs = 2 * 3 * part * part * order

    def shifted(value, k):
        return lax.ppermute(value, "dp", [(i, (i + k) % replicas) for i in range(replicas)])

    packed = call(
        pack_kernel, (like((blocks, slab, part), BF16),) * replicas, [place, grad_parts[0]], 1
    )
    arrived = [packed[0]] + [shifted(packed[k], k) for k in (1, 3, 2)]
    to_previous, to_next, to_far = call(
        root_pack_kernel,
        (like((2, part, 3 * part), BF16), like((2, part, 2 * part), BF16), like((2, part, part), BF16)),
        [place, root_left[0]],
        1,
    )
    arrived, to_previous, to_next, to_far = lax.optimization_barrier(
        (arrived, to_previous, to_next, to_far)
    )
    root_after = shifted(to_previous, 3)
    root_before = shifted(to_next, 1)
    root_far = shifted(to_far, 2)
    outgoing = call(
        sum_kernel, like((owners, slab, 2 * part), BF16), [block_owner, *arrived], 1
    )
    own = lax.all_to_all(outgoing, "fsdp", split_axis=0, concat_axis=0, tiled=True)
    own = own.reshape(order, 2 * part)
    own, root_after, root_before, root_far = lax.optimization_barrier(
        (own, root_after, root_before, root_far)
    )
    own = (own[:half], own[half:])

    before_top = shifted(own[0], 1)
    after_bottom = shifted(own[1], 3)
    before_bottom = shifted(own[1], 1)
    after_top = shifted(own[0], 3)
    far_top = shifted(before_top, 1)
    far_bottom = shifted(after_bottom, 3)

    root = root_right[0]
    own_square = call(square_kernel, like((8, 128)), [*own])
    stat = like((part, order))
    left, right = call(
        functools.partial(statistics_kernel, scale, (0,), True),
        (stat, stat),
        [place, *own, *own, left_stat[0], right_stat[0]],
        1,
        flops=2 * macs,
    )
    value = call(
        functools.partial(value_kernel, (0,), True),
        like((order, part)),
        [place, *own, root],
        1,
        flops=macs,
    )
    high, low = call(
        root_join_kernel,
        (like((order, order), BF16),) * 2,
        [place, root_left[0], root_after, root_before, root_far],
        1,
        cost=16 << 20,
    )
    near = (before_top, before_bottom, after_top, after_bottom)
    left, right = call(
        functools.partial(statistics_kernel, scale, (3, 1), False),
        (stat, stat),
        [place, *own, *near, left, right],
        1,
        flops=4 * macs,
    )
    value = call(
        functools.partial(value_kernel, (3, 1), False),
        like((order, part)),
        [place, *near, root, value],
        1,
        flops=2 * macs,
    )
    result, square, peak = call(
        functools.partial(result_kernel, 2),
        (like((order, part)), like((8, 128)), like((8, 128))),
        [place, far_top, far_bottom, root, value, high, low, own_square],
        1,
        flops=5 * macs,
    )
    squares = [square, shifted(square, 1), shifted(square, 3), shifted(square, 2)]
    codes = call(
        encode_kernel,
        like((owners, part * slab // 128, 128), BF16),
        [result, peak],
        cost=16 << 20,
    )
    codes = call(stamp_kernel, like((owners, part * slab // 128 + 8, 128), BF16), [peak, *squares, codes])
    returned = lax.all_to_all(codes, "fsdp", split_axis=0, concat_axis=0, tiled=True)
    left, right = call(
        functools.partial(statistics_kernel, scale, (2,), False),
        (stat, stat),
        [place, *own, far_top, far_bottom, left, right],
        1,
        flops=2 * macs,
    )
    direction = call(
        reorder_kernel, like((blocks, slab, part)), [block_owner, returned], 1
    )
    return (left[None], right[None], direction)


def solution(mesh):
    placed = (
        P("dp", None, "fsdp", None),
        P(),
        P("fsdp", "dp", None),
        P("fsdp", "dp", None),
        P("fsdp", "dp", None),
        P("fsdp", "dp", None),
    )
    return jax.shard_map(
        per_device,
        mesh=mesh,
        in_specs=placed,
        out_specs=(P("fsdp", "dp", None), P("fsdp", "dp", None), P(None, "fsdp", "dp")),
        check_vma=False,
    )
```

```python
import functools
import math

import jax
import jax.numpy as jnp
from jax import lax
from jax.experimental import pallas as pl
from jax.experimental.pallas import tpu as pltpu
from jax.sharding import PartitionSpec as P

AVERAGING = 0.9
GRAFT_EPS = 1e-06
VMEM_LIMIT = 24 * 1024 * 1024
STEPS = 1344
LARGEST = 252 * 128 + 127
FINE = 120.0

VMEM = pl.BlockSpec(memory_space=pltpu.VMEM)
SMEM = pl.BlockSpec(memory_space=pltpu.SMEM)
F32, BF16 = jnp.float32, jnp.bfloat16


def split(value):
    high = value.astype(BF16)
    low = (value - high.astype(F32)).astype(BF16)
    return high, low


def shrink(value):
    half = value.shape[1] // 2
    high = value.astype(BF16)
    wide = high.astype(F32)
    ratio = jnp.where(wide == 0.0, 0.0, (value - wide) / jnp.where(wide == 0.0, 1.0, wide))
    fine = jnp.clip(jnp.floor(ratio * (256.0 * FINE) + 0.5), -FINE, FINE)
    first, second = fine[:, :half], fine[:, half:]
    root = jnp.exp2(second * 0.5)
    word = (1.0 + jnp.abs(first) * (1.0 / 128.0)) * root * root
    return high, jnp.where(first < 0.0, -word, word).astype(BF16)


def widen(high, word):
    word = word.astype(F32)
    size = jnp.abs(word)
    second = jnp.floor(jnp.log(jnp.maximum(size, 1e-37)) * (1.0 / math.log(2.0)) + 0.01)
    root = jnp.exp2(second * -0.5)
    first = (size * root * root - 1.0) * 128.0
    first = jnp.where(word < 0.0, -first, first)
    fine = jnp.concatenate([first, second], axis=1) * (1.0 / (256.0 * FINE))
    return (high.astype(F32) * fine).astype(BF16)


def widen_kernel(part_ref, out_ref):
    size = out_ref.shape[1] // 2
    high = part_ref[:, :size]
    out_ref[:, :size] = high
    out_ref[:, size:] = widen(high, part_ref[:, size:])


def dot3(left, right, left_dim, right_dim):
    dims = (((left_dim,), (right_dim,)), ((), ()))

    def one(a, b):
        return lax.dot_general(a, b, dims, preferred_element_type=F32)

    return one(left[0], right[0]) + (one(left[0], right[1]) + one(left[1], right[0]))


def like(shape, dtype=F32):
    return jax.ShapeDtypeStruct(shape, dtype)


def call(kernel, outs, operands, n_smem=0, smem_outs=(), flops=0, cost=4 << 20):
    several = isinstance(outs, tuple)
    out_specs = tuple(
        SMEM if i in smem_outs else VMEM for i in range(len(outs) if several else 1)
    )
    return pl.pallas_call(
        kernel,
        out_shape=outs,
        in_specs=[SMEM] * n_smem + [VMEM] * (len(operands) - n_smem),
        out_specs=out_specs if several else out_specs[0],
        compiler_params=pltpu.CompilerParams(vmem_limit_bytes=VMEM_LIMIT),
        cost_estimate=pl.CostEstimate(flops=flops, bytes_accessed=cost, transcendentals=0),
    )(*operands)


def around(index, size, parts):
    return pl.ds(pl.multiple_of(lax.rem(index, parts) * size, size), size)


def pack_kernel(place_ref, grad_ref, *out_refs):
    part = out_refs[0].shape[2]
    parts = len(out_refs)
    for k, out_ref in enumerate(out_refs):
        out_ref[...] = grad_ref[:, :, around(place_ref[0] + k, part, parts)]


def sum_kernel(owner_ref, *refs):
    *replica_refs, out_ref = refs
    part = replica_refs[0].shape[2]
    out_ref[...] = jnp.zeros_like(out_ref)

    @pl.loop(0, replica_refs[0].shape[0], unroll=4)
    def _(b):
        total = replica_refs[0][b].astype(F32)
        for ref in replica_refs[1:]:
            total = total + ref[b].astype(F32)
        owner = owner_ref[b]
        out_ref[owner, :, :part], out_ref[owner, :, part:] = shrink(total)


def root_pack_kernel(place_ref, root_ref, next_ref, previous_ref, far_ref):
    size = root_ref.shape[0]
    parts = root_ref.shape[1] // size
    me = place_ref[0]

    def put(ref, slot, shift):
        high, word = shrink(root_ref[:, around(me + shift, size, parts)])
        ref[slot, :, :size] = high
        ref[slot, :, size:] = word

    for slot in range(3):
        put(next_ref, slot, slot)
    put(previous_ref, 0, 0)
    put(previous_ref, 1, parts - 1)
    put(far_ref, 0, 0)


def root_join_kernel(place_ref, root_ref, after_ref, before_ref, far_ref, high_ref, low_ref):
    size = root_ref.shape[0]
    parts = root_ref.shape[1] // size
    me = place_ref[0]

    def put(i, j, value):
        rows, columns = around(me + i, size, parts), around(me + j, size, parts)
        for ref, half in zip((high_ref, low_ref), value):
            ref[rows, columns] = half
            if i != j:
                ref[columns, rows] = half.astype(F32).T.astype(BF16)

    def block(ref, slot):
        high = ref[slot, :, :size]
        return high, widen(high, ref[slot, :, size:])

    for j in range(parts):
        put(0, j, split(root_ref[:, around(me + j, size, parts)]))
    put(1, 1, block(after_ref, 0))
    put(1, 2, block(after_ref, 1))
    put(1, 3, block(after_ref, 2))
    put(3, 3, block(before_ref, 0))
    put(3, 2, block(before_ref, 1))
    put(2, 2, block(far_ref, 0))


def own_half(refs, me, part):
    rows = pl.ds(pl.multiple_of(lax.rem(me, 2) * part, part), part)
    top, bottom = refs[0][rows, :], refs[1][rows, :]
    return jnp.where(me < 2, top, bottom)


def pair(value):
    part = value.shape[1] // 2
    return value[:, :part], value[:, part:]


def statistics_kernel(scale, shifts, first, place_ref, *refs):
    count = 2 * len(shifts)
    own, parts = refs[:2], refs[2 : 2 + count]
    left_in, right_in, left_out, right_out = refs[2 + count :]
    me = place_ref[0]
    part, order = left_in.shape
    half = order // 2
    keep = AVERAGING if first else 1.0
    right_out[...] = right_in[...] * keep
    left = left_in[...] * keep
    sums = [left[:, :half], left[:, half:]]
    for i, shift in enumerate(shifts):
        blocks = parts[2 * i : 2 * i + 2]
        mine = pair(own_half(blocks, me, part))
        halves = [pair(ref[...]) for ref in blocks]
        for h in range(2):
            sums[h] = sums[h] + scale * dot3(mine, halves[h], 1, 1)
        term = dot3(pair(own[0][...]), halves[0], 0, 0) + dot3(pair(own[1][...]), halves[1], 0, 0)
        columns = around(me + shift, part, order // part)
        right_out[:, columns] += scale * term
    left_out[:, :half] = sums[0]
    left_out[:, half:] = sums[1]


def value_terms(me, shifts, parts, root_ref):
    part, order = root_ref.shape
    sums = [None, None]
    for i, shift in enumerate(shifts):
        root = split(root_ref[:, around(me + shift, part, order // part)])
        for h in range(2):
            term = dot3(pair(parts[2 * i + h][...]), root, 1, 1)
            sums[h] = term if sums[h] is None else sums[h] + term
    return sums


def value_kernel(shifts, first, place_ref, *refs):
    count = 2 * len(shifts)
    parts, root_ref = refs[:count], refs[count]
    *value_in, value_out = refs[count + 1 :]
    half = value_out.shape[0] // 2
    sums = value_terms(place_ref[0], shifts, parts, root_ref)
    for h in range(2):
        rows = slice(h * half, (h + 1) * half)
        value_out[rows, :] = sums[h] if first else sums[h] + value_in[0][rows, :]


def square_kernel(top_ref, bottom_ref, out_ref):
    total = jnp.zeros((), F32)
    for ref in (top_ref, bottom_ref):
        high, low = pair(ref[...])
        whole = high.astype(F32) + low.astype(F32)
        total = total + jnp.sum(whole * whole)
    out_ref[...] = jnp.full(out_ref.shape, total)


def result_kernel(
    shift, place_ref, top_ref, bottom_ref, root_ref, value_ref, high_ref, low_ref, own_square, out_ref, square_ref, peak_ref
):
    order, part = value_ref.shape
    half = order // 2
    sums = value_terms(place_ref[0], (shift,), (top_ref, bottom_ref), root_ref)
    halves = [split(sums[h] + value_ref[h * half : (h + 1) * half, :]) for h in range(2)]
    value = [jnp.concatenate([halves[0][i], halves[1][i]], axis=0) for i in range(2)]
    total = jnp.zeros((), F32)
    peak = jnp.zeros((), F32)
    for i in range(order // part):
        rows = slice(i * part, (i + 1) * part)
        block = dot3((high_ref[rows, :], low_ref[rows, :]), value, 1, 0)
        out_ref[rows, :] = block
        total = total + jnp.sum(block * block)
        peak = jnp.maximum(peak, jnp.max(jnp.abs(block)))
    first = lax.broadcasted_iota(jnp.int32, square_ref.shape, 1) == 0
    square_ref[...] = jnp.where(first, own_square[...], total)
    peak_ref[...] = jnp.full(peak_ref.shape, peak)


def encode(ratio):
    size = jnp.abs(ratio)
    code = jnp.floor(jnp.log(jnp.maximum(size, 1e-30)) * (STEPS / math.log(2.0)) + (LARGEST + 0.5))
    code = jnp.minimum(code, float(LARGEST))
    exponent = jnp.floor(code * (1.0 / 128.0))
    root = jnp.exp2((exponent - 126.0) * 0.5)
    number = (1.0 + (code - exponent * 128.0) * (1.0 / 128.0)) * root * root
    number = jnp.where(code < 128.0, 0.0, number)
    return jnp.where(ratio < 0.0, -number, number).astype(BF16)


def decode(number):
    number = number.astype(F32)
    size = jnp.abs(number)
    exponent = jnp.floor(jnp.log(jnp.maximum(size, 2e-38)) * (1.0 / math.log(2.0)) + 0.002)
    root = jnp.exp2(exponent * -0.5)
    code = 128.0 * (exponent + 125.0 + size * root * root)
    value = jnp.exp2((code - LARGEST) * (1.0 / STEPS))
    value = jnp.where(size == 0.0, 0.0, value)
    return jnp.where(number < 0.0, -value, value)


def encode_kernel(value_ref, peak_ref, out_ref):
    slab = value_ref.shape[0] // out_ref.shape[0]
    lanes = out_ref.shape[2]
    peak = jnp.max(peak_ref[...])
    inverse = jnp.where(peak > 1e-37, 1.0 / jnp.maximum(peak, 1e-37), 0.0)
    pieces = value_ref.shape[1] // lanes

    @pl.loop(0, out_ref.shape[0], unroll=4)
    def _(o):
        rows = pl.ds(pl.multiple_of(o * slab, slab), slab)
        for i in range(pieces):
            value = value_ref[rows, i * lanes : (i + 1) * lanes]
            out_ref[o, i * slab : (i + 1) * slab, :] = encode(value * inverse)


def stamp_kernel(peak_ref, *refs):
    *square_refs, codes_ref, out_ref = refs
    total = square_refs[0][...]
    for ref in square_refs[1:]:
        total = total + ref[...]
    count, rows, lanes = out_ref.shape
    gradient, result = total[:, :1], total[:, 1:2]
    scale = peak_ref[...] * (jnp.sqrt(gradient) * lax.rsqrt(result + GRAFT_EPS))
    row = lax.broadcasted_iota(jnp.int32, scale.shape, 0)
    high = scale.astype(BF16).astype(F32)
    middle = (scale - high).astype(BF16).astype(F32)
    low = scale - high - middle
    value = jnp.where(row == 0, high, jnp.where(row == 1, middle, jnp.where(row == 2, low, 0.0)))
    tall = scale.shape[0]
    out_ref[:, : rows - tall, :] = codes_ref[...]
    out_ref[:, rows - tall :, :] = jnp.broadcast_to(value.astype(BF16)[None], (count, tall, lanes))


def reorder_kernel(owner_ref, returned_ref, out_ref):
    slab = out_ref.shape[1]
    rows, lanes = returned_ref.shape[1:]
    pieces = out_ref.shape[2] // lanes

    @pl.loop(0, out_ref.shape[0], unroll=4)
    def _(b):
        owner = owner_ref[b]
        scale = jnp.sum(returned_ref[owner, pieces * slab :, :].astype(F32), axis=0, keepdims=True)
        for i in range(pieces):
            value = decode(returned_ref[owner, i * slab : (i + 1) * slab, :])
            out_ref[b, :, i * lanes : (i + 1) * lanes] = value * scale


def per_device(grad_parts, block_owner, left_stat, right_stat, root_left, root_right):
    owners = lax.axis_size("fsdp")
    replicas = lax.axis_size("dp")
    me = lax.axis_index("dp")
    part, order = root_left.shape[1:]
    blocks, slab = grad_parts.shape[1:3]
    scale = (1.0 - AVERAGING) / order
    place = me.astype(jnp.int32).reshape(1)
    half = order // 2
    macs = 2 * 3 * part * part * order

    def shifted(value, k):
        return lax.ppermute(value, "dp", [(i, (i + k) % replicas) for i in range(replicas)])

    packed = call(
        pack_kernel, (like((blocks, slab, part), BF16),) * replicas, [place, grad_parts[0]], 1
    )
    arrived = [packed[0]] + [shifted(packed[k], k) for k in (1, 3, 2)]
    to_previous, to_next, to_far = call(
        root_pack_kernel,
        tuple(like((n, part, part // 2 * 3), BF16) for n in (3, 2, 1)),
        [place, root_left[0]],
        1,
    )
    arrived, to_previous, to_next, to_far = lax.optimization_barrier(
        (arrived, to_previous, to_next, to_far)
    )
    root_after = shifted(to_previous, 3)
    root_before = shifted(to_next, 1)
    root_far = shifted(to_far, 2)
    outgoing = call(
        sum_kernel, like((owners, slab, part // 2 * 3), BF16), [block_owner, *arrived], 1
    )
    own = lax.all_to_all(outgoing, "fsdp", split_axis=0, concat_axis=0, tiled=True)
    own = own.reshape(order, part // 2 * 3)
    own, root_after, root_before, root_far = lax.optimization_barrier(
        (own, root_after, root_before, root_far)
    )
    own = (own[:half], own[half:])

    before_top = shifted(own[0], 1)
    after_bottom = shifted(own[1], 3)
    before_bottom = shifted(own[1], 1)
    after_top = shifted(own[0], 3)
    far_top = shifted(before_top, 1)
    far_bottom = shifted(after_bottom, 3)

    def widened(value):
        return call(widen_kernel, like((half, 2 * part), BF16), [value])

    own = (widened(own[0]), widened(own[1]))
    before_top, before_bottom = widened(before_top), widened(before_bottom)
    after_top, after_bottom = widened(after_top), widened(after_bottom)
    far_top, far_bottom = widened(far_top), widened(far_bottom)
    root = root_right[0]
    own_square = call(square_kernel, like((8, 128)), [*own])
    stat = like((part, order))
    left, right = call(
        functools.partial(statistics_kernel, scale, (0,), True),
        (stat, stat),
        [place, *own, *own, left_stat[0], right_stat[0]],
        1,
        flops=2 * macs,
    )
    value = call(
        functools.partial(value_kernel, (0,), True),
        like((order, part)),
        [place, *own, root],
        1,
        flops=macs,
    )
    high, low = call(
        root_join_kernel,
        (like((order, order), BF16),) * 2,
        [place, root_left[0], root_after, root_before, root_far],
        1,
        cost=16 << 20,
    )
    near = (before_top, before_bottom, after_top, after_bottom)
    left, right = call(
        functools.partial(statistics_kernel, scale, (3, 1), False),
        (stat, stat),
        [place, *own, *near, left, right],
        1,
        flops=4 * macs,
    )
    value = call(
        functools.partial(value_kernel, (3, 1), False),
        like((order, part)),
        [place, *near, root, value],
        1,
        flops=2 * macs,
    )
    result, square, peak = call(
        functools.partial(result_kernel, 2),
        (like((order, part)), like((8, 128)), like((8, 128))),
        [place, far_top, far_bottom, root, value, high, low, own_square],
        1,
        flops=5 * macs,
    )
    squares = [square, shifted(square, 1), shifted(square, 3), shifted(square, 2)]
    codes = call(
        encode_kernel,
        like((owners, part * slab // 128, 128), BF16),
        [result, peak],
        cost=16 << 20,
    )
    codes = call(stamp_kernel, like((owners, part * slab // 128 + 8, 128), BF16), [peak, *squares, codes])
    returned = lax.all_to_all(codes, "fsdp", split_axis=0, concat_axis=0, tiled=True)
    left, right = call(
        functools.partial(statistics_kernel, scale, (2,), False),
        (stat, stat),
        [place, *own, far_top, far_bottom, left, right],
        1,
        flops=2 * macs,
    )
    direction = call(
        reorder_kernel, like((blocks, slab, part)), [block_owner, returned], 1
    )
    return (left[None], right[None], direction)


def solution(mesh):
    placed = (
        P("dp", None, "fsdp", None),
        P(),
        P("fsdp", "dp", None),
        P("fsdp", "dp", None),
        P("fsdp", "dp", None),
        P("fsdp", "dp", None),
    )
    return jax.shard_map(
        per_device,
        mesh=mesh,
        in_specs=placed,
        out_specs=(P("fsdp", "dp", None), P("fsdp", "dp", None), P(None, "fsdp", "dp")),
        check_vma=False,
    )
```

```python
import functools
import math

import jax
import jax.numpy as jnp
from jax import lax
from jax.experimental import pallas as pl
from jax.experimental.pallas import tpu as pltpu
from jax.sharding import PartitionSpec as P

AVERAGING = 0.9
GRAFT_EPS = 1e-06
VMEM_LIMIT = 24 * 1024 * 1024
STEPS = 1344
LARGEST = 252 * 128 + 127
FINE = 120.0

VMEM = pl.BlockSpec(memory_space=pltpu.VMEM)
SMEM = pl.BlockSpec(memory_space=pltpu.SMEM)
F32, BF16 = jnp.float32, jnp.bfloat16


def split(value):
    high = value.astype(BF16)
    low = (value - high.astype(F32)).astype(BF16)
    return high, low


def shrink(value):
    half = value.shape[1] // 2
    high = value.astype(BF16)
    wide = high.astype(F32)
    inverse = pl.reciprocal(jnp.where(wide == 0.0, 1.0, wide), approx=True)
    ratio = jnp.where(wide == 0.0, 0.0, (value - wide) * inverse)
    fine = jnp.clip(jnp.floor(ratio * (256.0 * FINE) + 0.5), -FINE, FINE)
    first, second = fine[:, :half], fine[:, half:]
    root = jnp.exp2(second * 0.5)
    word = (1.0 + jnp.abs(first) * (1.0 / 128.0)) * root * root
    return high, jnp.where(first < 0.0, -word, word).astype(BF16)


def widen(high, word):
    word = word.astype(F32)
    size = jnp.abs(word)
    second = jnp.floor(jnp.log(jnp.maximum(size, 1e-37)) * (1.0 / math.log(2.0)) + 0.01)
    root = jnp.exp2(second * -0.5)
    first = (size * root * root - 1.0) * 128.0
    first = jnp.where(word < 0.0, -first, first)
    fine = jnp.concatenate([first, second], axis=1) * (1.0 / (256.0 * FINE))
    return (high.astype(F32) * fine).astype(BF16)


def halves_kernel(whole_ref, top_ref, bottom_ref):
    half = top_ref.shape[0]
    top_ref[...] = whole_ref[:half, :]
    bottom_ref[...] = whole_ref[half:, :]


def widen_kernel(part_ref, out_ref):
    size = out_ref.shape[1] // 2
    high = part_ref[:, :size]
    out_ref[:, :size] = high
    out_ref[:, size:] = widen(high, part_ref[:, size:])


def dot3(left, right, left_dim, right_dim):
    dims = (((left_dim,), (right_dim,)), ((), ()))

    def one(a, b):
        return lax.dot_general(a, b, dims, preferred_element_type=F32)

    return one(left[0], right[0]) + (one(left[0], right[1]) + one(left[1], right[0]))


def like(shape, dtype=F32):
    return jax.ShapeDtypeStruct(shape, dtype)


def call(kernel, outs, operands, n_smem=0, smem_outs=(), flops=0, cost=4 << 20):
    several = isinstance(outs, tuple)
    out_specs = tuple(
        SMEM if i in smem_outs else VMEM for i in range(len(outs) if several else 1)
    )
    return pl.pallas_call(
        kernel,
        out_shape=outs,
        in_specs=[SMEM] * n_smem + [VMEM] * (len(operands) - n_smem),
        out_specs=out_specs if several else out_specs[0],
        compiler_params=pltpu.CompilerParams(vmem_limit_bytes=VMEM_LIMIT),
        cost_estimate=pl.CostEstimate(flops=flops, bytes_accessed=cost, transcendentals=0),
    )(*operands)


def around(index, size, parts):
    return pl.ds(pl.multiple_of(lax.rem(index, parts) * size, size), size)


def pack_kernel(place_ref, grad_ref, *out_refs):
    part = out_refs[0].shape[2]
    parts = len(out_refs)
    for k, out_ref in enumerate(out_refs):
        out_ref[...] = grad_ref[:, :, around(place_ref[0] + k, part, parts)]


def sum_kernel(owner_ref, *refs):
    *replica_refs, out_ref = refs
    part = replica_refs[0].shape[2]
    out_ref[...] = jnp.zeros_like(out_ref)

    @pl.loop(0, replica_refs[0].shape[0], unroll=8)
    def _(b):
        total = replica_refs[0][b].astype(F32)
        for ref in replica_refs[1:]:
            total = total + ref[b].astype(F32)
        owner = owner_ref[b]
        out_ref[owner, :, :part], out_ref[owner, :, part:] = shrink(total)


def root_pack_kernel(place_ref, root_ref, next_ref, previous_ref):
    size = root_ref.shape[0]
    parts = root_ref.shape[1] // size
    me = place_ref[0]

    def put(ref, slot, shift):
        high, word = shrink(root_ref[:, around(me + shift, size, parts)])
        ref[slot, :, :size] = high
        ref[slot, :, size:] = word

    for slot in range(3):
        put(next_ref, slot, slot)
    put(previous_ref, 0, 0)
    put(previous_ref, 1, parts - 1)


def root_join_kernel(place_ref, root_ref, after_ref, before_ref, far_ref, high_ref, low_ref):
    size = root_ref.shape[0]
    parts = root_ref.shape[1] // size
    me = place_ref[0]

    def put(i, j, value):
        rows, columns = around(me + i, size, parts), around(me + j, size, parts)
        for ref, half in zip((high_ref, low_ref), value):
            ref[rows, columns] = half
            if i != j:
                ref[columns, rows] = half.astype(F32).T.astype(BF16)

    def block(ref, slot):
        high = ref[slot, :, :size]
        return high, widen(high, ref[slot, :, size:])

    for j in range(parts):
        put(0, j, split(root_ref[:, around(me + j, size, parts)]))
    put(1, 1, block(after_ref, 0))
    put(1, 2, block(after_ref, 1))
    put(1, 3, block(after_ref, 2))
    put(3, 3, block(before_ref, 0))
    put(3, 2, block(before_ref, 1))
    put(2, 2, block(far_ref, 0))


def own_half(refs, me, part):
    rows = pl.ds(pl.multiple_of(lax.rem(me, 2) * part, part), part)
    top, bottom = refs[0][rows, :], refs[1][rows, :]
    return jnp.where(me < 2, top, bottom)


def pair(value):
    part = value.shape[1] // 2
    return value[:, :part], value[:, part:]


def statistics_kernel(scale, shifts, first, place_ref, *refs):
    count = 2 * len(shifts)
    own, parts = refs[:2], refs[2 : 2 + count]
    left_in, right_in, left_out, right_out = refs[2 + count :]
    me = place_ref[0]
    part, order = left_in.shape
    half = order // 2
    keep = AVERAGING if first else 1.0
    right_out[...] = right_in[...] * keep
    left = left_in[...] * keep
    sums = [left[:, :half], left[:, half:]]
    for i, shift in enumerate(shifts):
        blocks = parts[2 * i : 2 * i + 2]
        mine = pair(own_half(blocks, me, part))
        halves = [pair(ref[...]) for ref in blocks]
        for h in range(2):
            sums[h] = sums[h] + scale * dot3(mine, halves[h], 1, 1)
        term = dot3(pair(own[0][...]), halves[0], 0, 0) + dot3(pair(own[1][...]), halves[1], 0, 0)
        columns = around(me + shift, part, order // part)
        right_out[:, columns] += scale * term
    left_out[:, :half] = sums[0]
    left_out[:, half:] = sums[1]


def value_terms(me, shifts, parts, root_ref):
    part, order = root_ref.shape
    sums = [None, None]
    for i, shift in enumerate(shifts):
        root = split(root_ref[:, around(me + shift, part, order // part)])
        for h in range(2):
            term = dot3(parts[2 * i + h], root, 1, 1)
            sums[h] = term if sums[h] is None else sums[h] + term
    return sums


def value_kernel(shifts, first, place_ref, *refs):
    count = 2 * len(shifts)
    parts, root_ref = refs[:count], refs[count]
    *value_in, value_out = refs[count + 1 :]
    half = value_out.shape[0] // 2
    sums = value_terms(place_ref[0], shifts, [pair(ref[...]) for ref in parts], root_ref)
    for h in range(2):
        rows = slice(h * half, (h + 1) * half)
        value_out[rows, :] = sums[h] if first else sums[h] + value_in[0][rows, :]


def square_kernel(top_ref, bottom_ref, out_ref):
    total = jnp.zeros((), F32)
    for ref in (top_ref, bottom_ref):
        high, low = pair(ref[...])
        whole = high.astype(F32) + low.astype(F32)
        total = total + jnp.sum(whole * whole)
    out_ref[...] = jnp.full(out_ref.shape, total)


def result_kernel(
    shift, place_ref, top_ref, bottom_ref, root_ref, value_ref, high_ref, low_ref, own_square, out_ref, square_ref, peak_ref
):
    order, part = value_ref.shape
    half = order // 2
    coded = [(ref[:, :part], ref[:, part:]) for ref in (top_ref, bottom_ref)]
    pieces = [(high, widen(high, word)) for high, word in coded]
    sums = value_terms(place_ref[0], (shift,), pieces, root_ref)
    halves = [split(sums[h] + value_ref[h * half : (h + 1) * half, :]) for h in range(2)]
    value = [jnp.concatenate([halves[0][i], halves[1][i]], axis=0) for i in range(2)]
    total = jnp.zeros((), F32)
    peak = jnp.zeros((), F32)
    for i in range(2):
        rows = slice(i * half, (i + 1) * half)
        block = dot3((high_ref[rows, :], low_ref[rows, :]), value, 1, 0)
        out_ref[rows, :] = block
        total = total + jnp.sum(block * block)
        peak = jnp.maximum(peak, jnp.max(jnp.abs(block)))
    first = lax.broadcasted_iota(jnp.int32, square_ref.shape, 1) == 0
    square_ref[...] = jnp.where(first, own_square[...], total)
    peak_ref[...] = jnp.full(peak_ref.shape, peak)


def encode(ratio):
    size = jnp.abs(ratio)
    code = jnp.floor(jnp.log(jnp.maximum(size, 1e-30)) * (STEPS / math.log(2.0)) + (LARGEST + 0.5))
    code = jnp.minimum(code, float(LARGEST))
    exponent = jnp.floor(code * (1.0 / 128.0))
    root = jnp.exp2((exponent - 126.0) * 0.5)
    number = (1.0 + (code - exponent * 128.0) * (1.0 / 128.0)) * root * root
    number = jnp.where(code < 128.0, 0.0, number)
    return jnp.where(ratio < 0.0, -number, number).astype(BF16)


def decode(number):
    number = number.astype(F32)
    size = jnp.abs(number)
    exponent = jnp.floor(jnp.log(jnp.maximum(size, 2e-38)) * (1.0 / math.log(2.0)) + 0.002)
    root = jnp.exp2(exponent * -0.5)
    code = 128.0 * (exponent + 125.0 + size * root * root)
    value = jnp.exp2((code - LARGEST) * (1.0 / STEPS))
    value = jnp.where(size == 0.0, 0.0, value)
    return jnp.where(number < 0.0, -value, value)


def encode_kernel(value_ref, peak_ref, out_ref):
    slab = value_ref.shape[0] // out_ref.shape[0]
    lanes = out_ref.shape[2]
    peak = jnp.max(peak_ref[...])
    inverse = jnp.where(peak > 1e-37, 1.0 / jnp.maximum(peak, 1e-37), 0.0)
    pieces = value_ref.shape[1] // lanes

    @pl.loop(0, out_ref.shape[0], unroll=16)
    def _(o):
        rows = pl.ds(pl.multiple_of(o * slab, slab), slab)
        for i in range(pieces):
            value = value_ref[rows, i * lanes : (i + 1) * lanes]
            out_ref[o, i * slab : (i + 1) * slab, :] = encode(value * inverse)


def stamp_kernel(peak_ref, *refs):
    *square_refs, codes_ref, out_ref = refs
    total = square_refs[0][...]
    for ref in square_refs[1:]:
        total = total + ref[...]
    count, rows, lanes = out_ref.shape
    gradient, result = total[:, :1], total[:, 1:2]
    scale = peak_ref[...] * (jnp.sqrt(gradient) * lax.rsqrt(result + GRAFT_EPS))
    row = lax.broadcasted_iota(jnp.int32, scale.shape, 0)
    high = scale.astype(BF16).astype(F32)
    middle = (scale - high).astype(BF16).astype(F32)
    low = scale - high - middle
    value = jnp.where(row == 0, high, jnp.where(row == 1, middle, jnp.where(row == 2, low, 0.0)))
    tall = scale.shape[0]
    out_ref[:, : rows - tall, :] = codes_ref[...]
    out_ref[:, rows - tall :, :] = jnp.broadcast_to(value.astype(BF16)[None], (count, tall, lanes))


def reorder_kernel(owner_ref, returned_ref, out_ref):
    slab = out_ref.shape[1]
    rows, lanes = returned_ref.shape[1:]
    pieces = out_ref.shape[2] // lanes

    @pl.loop(0, out_ref.shape[0], unroll=16)
    def _(b):
        owner = owner_ref[b]
        scale = jnp.sum(returned_ref[owner, pieces * slab :, :].astype(F32), axis=0, keepdims=True)
        for i in range(pieces):
            value = decode(returned_ref[owner, i * slab : (i + 1) * slab, :])
            out_ref[b, :, i * lanes : (i + 1) * lanes] = value * scale


def per_device(grad_parts, block_owner, left_stat, right_stat, root_left, root_right):
    owners = lax.axis_size("fsdp")
    replicas = lax.axis_size("dp")
    me = lax.axis_index("dp")
    part, order = root_left.shape[1:]
    blocks, slab = grad_parts.shape[1:3]
    scale = (1.0 - AVERAGING) / order
    place = me.astype(jnp.int32).reshape(1)
    half = order // 2
    macs = 2 * 3 * part * part * order

    def shifted(value, k):
        return lax.ppermute(value, "dp", [(i, (i + k) % replicas) for i in range(replicas)])

    packed = call(
        pack_kernel,
        (like((blocks, slab, part), BF16),) * replicas,
        [place, grad_parts[0]],
        1,
    )
    arrived = [packed[0]] + [shifted(packed[k], k) for k in (1, 3, 2)]
    to_previous, to_next = call(
        root_pack_kernel,
        tuple(like((n, part, part // 2 * 3), BF16) for n in (3, 2)),
        [place, root_left[0]],
        1,
    )
    arrived, to_previous, to_next = lax.optimization_barrier((arrived, to_previous, to_next))
    root_after = shifted(to_previous, 3)
    root_before = shifted(to_next, 1)
    root_far = shifted(root_before[:1], 1)
    outgoing = call(
        sum_kernel, like((owners, slab, part // 2 * 3), BF16), [block_owner, *arrived], 1
    )
    own = lax.all_to_all(outgoing, "fsdp", split_axis=0, concat_axis=0, tiled=True)
    own = own.reshape(order, part // 2 * 3)
    own, root_after, root_before, root_far = lax.optimization_barrier(
        (own, root_after, root_before, root_far)
    )
    own = call(halves_kernel, (like((half, part // 2 * 3), BF16),) * 2, [own])

    before_top = shifted(own[0], 1)
    after_bottom = shifted(own[1], 3)
    before_bottom = shifted(own[1], 1)
    after_top = shifted(own[0], 3)
    far_top = shifted(before_top, 1)
    far_bottom = shifted(after_bottom, 3)

    def widened(value):
        return call(widen_kernel, like((half, 2 * part), BF16), [value])

    own = (widened(own[0]), widened(own[1]))
    before_top, before_bottom = widened(before_top), widened(before_bottom)
    after_top, after_bottom = widened(after_top), widened(after_bottom)
    root = root_right[0]
    own_square = call(square_kernel, like((8, 128)), [*own])
    stat = like((part, order))
    left, right = call(
        functools.partial(statistics_kernel, scale, (0,), True),
        (stat, stat),
        [place, *own, *own, left_stat[0], right_stat[0]],
        1,
        flops=2 * macs,
    )
    value = call(
        functools.partial(value_kernel, (0,), True),
        like((order, part)),
        [place, *own, root],
        1,
        flops=macs,
    )
    high, low = call(
        root_join_kernel,
        (like((order, order), BF16),) * 2,
        [place, root_left[0], root_after, root_before, root_far],
        1,
        cost=16 << 20,
    )
    near = (before_top, before_bottom, after_top, after_bottom)
    left, right = call(
        functools.partial(statistics_kernel, scale, (3, 1), False),
        (stat, stat),
        [place, *own, *near, left, right],
        1,
        flops=4 * macs,
    )
    value = call(
        functools.partial(value_kernel, (3, 1), False),
        like((order, part)),
        [place, *near, root, value],
        1,
        flops=2 * macs,
    )
    result, square, peak = call(
        functools.partial(result_kernel, 2),
        (like((order, part)), like((8, 128)), like((8, 128))),
        [place, far_top, far_bottom, root, value, high, low, own_square],
        1,
        flops=5 * macs,
    )
    squares = [square, shifted(square, 1), shifted(square, 3), shifted(square, 2)]
    codes = call(
        encode_kernel,
        like((owners, part * slab // 128, 128), BF16),
        [result, peak],
        cost=16 << 20,
    )
    codes = call(stamp_kernel, like((owners, part * slab // 128 + 8, 128), BF16), [peak, *squares, codes])
    returned = lax.all_to_all(codes, "fsdp", split_axis=0, concat_axis=0, tiled=True)
    left, right = call(
        functools.partial(statistics_kernel, scale, (2,), False),
        (stat, stat),
        [place, *own, widened(far_top), widened(far_bottom), left, right],
        1,
        flops=2 * macs,
    )
    direction = call(
        reorder_kernel, like((blocks, slab, part)), [block_owner, returned], 1
    )
    return (left[None], right[None], direction)


def solution(mesh):
    placed = (
        P("dp", None, "fsdp", None),
        P(),
        P("fsdp", "dp", None),
        P("fsdp", "dp", None),
        P("fsdp", "dp", None),
        P("fsdp", "dp", None),
    )
    return jax.shard_map(
        per_device,
        mesh=mesh,
        in_specs=placed,
        out_specs=(P("fsdp", "dp", None), P("fsdp", "dp", None), P(None, "fsdp", "dp")),
        check_vma=False,
    )
```

```python
import functools
import math

import jax
import jax.numpy as jnp
from jax import lax
from jax.experimental import pallas as pl
from jax.experimental.pallas import tpu as pltpu
from jax.sharding import PartitionSpec as P

AVERAGING = 0.9
GRAFT_EPS = 1e-06
VMEM_LIMIT = 24 * 1024 * 1024
STEPS = 1344
LARGEST = 252 * 128 + 127
FINE = 120.0

VMEM = pl.BlockSpec(memory_space=pltpu.VMEM)
SMEM = pl.BlockSpec(memory_space=pltpu.SMEM)
F32, BF16 = jnp.float32, jnp.bfloat16


def split(value):
    high = value.astype(BF16)
    low = (value - high.astype(F32)).astype(BF16)
    return high, low


def shrink(value):
    half = value.shape[1] // 2
    high = value.astype(BF16)
    wide = high.astype(F32)
    inverse = pl.reciprocal(jnp.where(wide == 0.0, 1.0, wide), approx=True)
    ratio = jnp.where(wide == 0.0, 0.0, (value - wide) * inverse)
    fine = jnp.clip(jnp.floor(ratio * (256.0 * FINE) + 0.5), -FINE, FINE)
    first, second = fine[:, :half], fine[:, half:]
    root = jnp.exp2(second * 0.5)
    word = (1.0 + jnp.abs(first) * (1.0 / 128.0)) * root * root
    return high, jnp.where(first < 0.0, -word, word).astype(BF16)


def widen(high, word):
    word = word.astype(F32)
    size = jnp.abs(word)
    second = jnp.floor(jnp.log(jnp.maximum(size, 1e-37)) * (1.0 / math.log(2.0)) + 0.01)
    root = jnp.exp2(second * -0.5)
    first = (size * root * root - 1.0) * 128.0
    first = jnp.where(word < 0.0, -first, first)
    fine = jnp.concatenate([first, second], axis=1) * (1.0 / (256.0 * FINE))
    return (high.astype(F32) * fine).astype(BF16)


def halves_kernel(whole_ref, top_ref, bottom_ref):
    half = top_ref.shape[0]
    top_ref[...] = whole_ref[:half, :]
    bottom_ref[...] = whole_ref[half:, :]


def widen_kernel(part_ref, out_ref):
    size = out_ref.shape[1] // 2
    high = part_ref[:, :size]
    out_ref[:, :size] = high
    out_ref[:, size:] = widen(high, part_ref[:, size:])


def dot3(left, right, left_dim, right_dim):
    dims = (((left_dim,), (right_dim,)), ((), ()))

    def one(a, b):
        return lax.dot_general(a, b, dims, preferred_element_type=F32)

    return one(left[0], right[0]) + (one(left[0], right[1]) + one(left[1], right[0]))


def like(shape, dtype=F32):
    return jax.ShapeDtypeStruct(shape, dtype)


def call(kernel, outs, operands, n_smem=0, smem_outs=(), flops=0, cost=4 << 20):
    several = isinstance(outs, tuple)
    out_specs = tuple(
        SMEM if i in smem_outs else VMEM for i in range(len(outs) if several else 1)
    )
    return pl.pallas_call(
        kernel,
        out_shape=outs,
        in_specs=[SMEM] * n_smem + [VMEM] * (len(operands) - n_smem),
        out_specs=out_specs if several else out_specs[0],
        compiler_params=pltpu.CompilerParams(vmem_limit_bytes=VMEM_LIMIT),
        cost_estimate=pl.CostEstimate(flops=flops, bytes_accessed=cost, transcendentals=0),
    )(*operands)


def around(index, size, parts):
    return pl.ds(pl.multiple_of(lax.rem(index, parts) * size, size), size)


def pack_kernel(place_ref, grad_ref, *out_refs):
    part = out_refs[0].shape[2]
    parts = len(out_refs)
    for k, out_ref in enumerate(out_refs):
        out_ref[...] = grad_ref[:, :, around(place_ref[0] + k, part, parts)]


def sum_kernel(owner_ref, *refs):
    *replica_refs, out_ref = refs
    part = replica_refs[0].shape[2]
    out_ref[...] = jnp.zeros_like(out_ref)

    @pl.loop(0, replica_refs[0].shape[0], unroll=8)
    def _(b):
        total = replica_refs[0][b].astype(F32)
        for ref in replica_refs[1:]:
            total = total + ref[b].astype(F32)
        owner = owner_ref[b]
        out_ref[owner, :, :part], out_ref[owner, :, part:] = shrink(total)


def root_pack_kernel(place_ref, root_ref, next_ref, previous_ref):
    size = root_ref.shape[0]
    parts = root_ref.shape[1] // size
    me = place_ref[0]

    def put(ref, slot, shift):
        high, word = shrink(root_ref[:, around(me + shift, size, parts)])
        ref[slot, :, :size] = high
        ref[slot, :, size:] = word

    for slot in range(3):
        put(next_ref, slot, slot)
    put(previous_ref, 0, 0)
    put(previous_ref, 1, parts - 1)


def root_join_kernel(place_ref, root_ref, after_ref, before_ref, far_ref, high_ref, low_ref):
    size = root_ref.shape[0]
    parts = root_ref.shape[1] // size
    me = place_ref[0]

    def put(i, j, value):
        rows, columns = around(me + i, size, parts), around(me + j, size, parts)
        for ref, half in zip((high_ref, low_ref), value):
            ref[rows, columns] = half
            if i != j:
                ref[columns, rows] = half.astype(F32).T.astype(BF16)

    def block(ref, slot):
        high = ref[slot, :, :size]
        return high, widen(high, ref[slot, :, size:])

    for j in range(parts):
        put(0, j, split(root_ref[:, around(me + j, size, parts)]))
    put(1, 1, block(after_ref, 0))
    put(1, 2, block(after_ref, 1))
    put(1, 3, block(after_ref, 2))
    put(3, 3, block(before_ref, 0))
    put(3, 2, block(before_ref, 1))
    put(2, 2, block(far_ref, 0))


def own_half(refs, me, part):
    rows = pl.ds(pl.multiple_of(lax.rem(me, 2) * part, part), part)
    top, bottom = refs[0][rows, :], refs[1][rows, :]
    return jnp.where(me < 2, top, bottom)


def pair(value):
    part = value.shape[1] // 2
    return value[:, :part], value[:, part:]


def statistics_kernel(scale, shifts, first, place_ref, *refs):
    count = 2 * len(shifts)
    own, parts = refs[:2], refs[2 : 2 + count]
    left_in, right_in, left_out, right_out = refs[2 + count :]
    me = place_ref[0]
    part, order = left_in.shape
    half = order // 2
    keep = AVERAGING if first else 1.0
    right_out[...] = right_in[...] * keep
    left = left_in[...] * keep
    sums = [left[:, :half], left[:, half:]]
    for i, shift in enumerate(shifts):
        blocks = parts[2 * i : 2 * i + 2]
        mine = pair(own_half(blocks, me, part))
        halves = [pair(ref[...]) for ref in blocks]
        for h in range(2):
            sums[h] = sums[h] + scale * dot3(mine, halves[h], 1, 1)
        term = dot3(pair(own[0][...]), halves[0], 0, 0) + dot3(pair(own[1][...]), halves[1], 0, 0)
        columns = around(me + shift, part, order // part)
        right_out[:, columns] += scale * term
    left_out[:, :half] = sums[0]
    left_out[:, half:] = sums[1]


def value_terms(me, shifts, parts, root_ref):
    part, order = root_ref.shape
    sums = [None, None]
    for i, shift in enumerate(shifts):
        root = split(root_ref[:, around(me + shift, part, order // part)])
        for h in range(2):
            term = dot3(parts[2 * i + h], root, 1, 1)
            sums[h] = term if sums[h] is None else sums[h] + term
    return sums


def value_kernel(shifts, first, place_ref, *refs):
    count = 2 * len(shifts)
    parts, root_ref = refs[:count], refs[count]
    *value_in, value_out = refs[count + 1 :]
    half = value_out.shape[0] // 2
    sums = value_terms(place_ref[0], shifts, [pair(ref[...]) for ref in parts], root_ref)
    for h in range(2):
        rows = slice(h * half, (h + 1) * half)
        value_out[rows, :] = sums[h] if first else sums[h] + value_in[0][rows, :]


def square_kernel(top_ref, bottom_ref, out_ref):
    total = jnp.zeros((), F32)
    for ref in (top_ref, bottom_ref):
        high, low = pair(ref[...])
        whole = high.astype(F32) + low.astype(F32)
        total = total + jnp.sum(whole * whole)
    out_ref[...] = jnp.full(out_ref.shape, total)


def result_kernel(
    shift, place_ref, top_ref, bottom_ref, root_ref, value_ref, high_ref, low_ref, own_square, out_ref, square_ref, peak_ref
):
    order, part = value_ref.shape
    half = order // 2
    coded = [(ref[:, :part], ref[:, part:]) for ref in (top_ref, bottom_ref)]
    pieces = [(high, widen(high, word)) for high, word in coded]
    sums = value_terms(place_ref[0], (shift,), pieces, root_ref)
    halves = [split(sums[h] + value_ref[h * half : (h + 1) * half, :]) for h in range(2)]
    value = [jnp.concatenate([halves[0][i], halves[1][i]], axis=0) for i in range(2)]
    total = jnp.zeros((), F32)
    peak = jnp.zeros((), F32)
    for i in range(2):
        rows = slice(i * half, (i + 1) * half)
        block = dot3((high_ref[rows, :], low_ref[rows, :]), value, 1, 0)
        out_ref[rows, :] = block
        total = total + jnp.sum(block * block)
        peak = jnp.maximum(peak, jnp.max(jnp.abs(block)))
    first = lax.broadcasted_iota(jnp.int32, square_ref.shape, 1) == 0
    square_ref[...] = jnp.where(first, own_square[...], total)
    peak_ref[...] = jnp.full(peak_ref.shape, peak)


def encode(ratio):
    size = jnp.abs(ratio)
    code = jnp.floor(jnp.log(jnp.maximum(size, 1e-30)) * (STEPS / math.log(2.0)) + (LARGEST + 0.5))
    code = jnp.minimum(code, float(LARGEST))
    exponent = jnp.floor(code * (1.0 / 128.0))
    root = jnp.exp2((exponent - 126.0) * 0.5)
    number = (1.0 + (code - exponent * 128.0) * (1.0 / 128.0)) * root * root
    number = jnp.where(code < 128.0, 0.0, number)
    return jnp.where(ratio < 0.0, -number, number).astype(BF16)


def decode(number):
    number = number.astype(F32)
    size = jnp.abs(number)
    exponent = jnp.floor(jnp.log(jnp.maximum(size, 2e-38)) * (1.0 / math.log(2.0)) + 0.002)
    root = jnp.exp2(exponent * -0.5)
    code = 128.0 * (exponent + 125.0 + size * root * root)
    value = jnp.exp2((code - LARGEST) * (1.0 / STEPS))
    value = jnp.where(size == 0.0, 0.0, value)
    return jnp.where(number < 0.0, -value, value)


def encode_kernel(value_ref, peak_ref, out_ref):
    slab = value_ref.shape[0] // out_ref.shape[0]
    lanes = out_ref.shape[2]
    peak = jnp.max(peak_ref[...])
    inverse = jnp.where(peak > 1e-37, 1.0 / jnp.maximum(peak, 1e-37), 0.0)
    pieces = value_ref.shape[1] // lanes

    @pl.loop(0, out_ref.shape[0], unroll=16)
    def _(o):
        rows = pl.ds(pl.multiple_of(o * slab, slab), slab)
        for i in range(pieces):
            value = value_ref[rows, i * lanes : (i + 1) * lanes]
            out_ref[o, i * slab : (i + 1) * slab, :] = encode(value * inverse)


def stamp_kernel(peak_ref, *refs):
    *square_refs, codes_ref, out_ref = refs
    total = square_refs[0][...]
    for ref in square_refs[1:]:
        total = total + ref[...]
    count, rows, lanes = out_ref.shape
    gradient, result = total[:, :1], total[:, 1:2]
    scale = peak_ref[...] * (jnp.sqrt(gradient) * lax.rsqrt(result + GRAFT_EPS))
    row = lax.broadcasted_iota(jnp.int32, scale.shape, 0)
    high = scale.astype(BF16).astype(F32)
    middle = (scale - high).astype(BF16).astype(F32)
    low = scale - high - middle
    value = jnp.where(row == 0, high, jnp.where(row == 1, middle, jnp.where(row == 2, low, 0.0)))
    tall = scale.shape[0]
    out_ref[:, : rows - tall, :] = codes_ref[...]
    out_ref[:, rows - tall :, :] = jnp.broadcast_to(value.astype(BF16)[None], (count, tall, lanes))


def reorder_kernel(owner_ref, returned_ref, out_ref):
    slab = out_ref.shape[1]
    rows, lanes = returned_ref.shape[1:]
    pieces = out_ref.shape[2] // lanes

    @pl.loop(0, out_ref.shape[0], unroll=16)
    def _(b):
        owner = owner_ref[b]
        scale = jnp.sum(returned_ref[owner, pieces * slab :, :].astype(F32), axis=0, keepdims=True)
        for i in range(pieces):
            value = decode(returned_ref[owner, i * slab : (i + 1) * slab, :])
            out_ref[b, :, i * lanes : (i + 1) * lanes] = value * scale


def per_device(grad_parts, block_owner, left_stat, right_stat, root_left, root_right):
    owners = lax.axis_size("fsdp")
    replicas = lax.axis_size("dp")
    me = lax.axis_index("dp")
    part, order = root_left.shape[1:]
    blocks, slab = grad_parts.shape[1:3]
    scale = (1.0 - AVERAGING) / order
    place = me.astype(jnp.int32).reshape(1)
    half = order // 2
    macs = 2 * 3 * part * part * order

    def shifted(value, k):
        return lax.ppermute(value, "dp", [(i, (i + k) % replicas) for i in range(replicas)])

    packed = call(
        pack_kernel,
        (like((blocks, slab, part), BF16),) * replicas,
        [place, grad_parts[0]],
        1,
    )
    arrived = [packed[0]] + [shifted(packed[k], k) for k in (2, 1, 3)]
    to_previous, to_next = call(
        root_pack_kernel,
        tuple(like((n, part, part // 2 * 3), BF16) for n in (3, 2)),
        [place, root_left[0]],
        1,
    )
    arrived, to_previous, to_next = lax.optimization_barrier((arrived, to_previous, to_next))
    root_after = shifted(to_previous, 3)
    root_before = shifted(to_next, 1)
    root_far = shifted(root_before[:1], 1)
    outgoing = call(
        sum_kernel, like((owners, slab, part // 2 * 3), BF16), [block_owner, *arrived], 1
    )
    own = lax.all_to_all(outgoing, "fsdp", split_axis=0, concat_axis=0, tiled=True)
    own = own.reshape(order, part // 2 * 3)
    own, root_after, root_before, root_far = lax.optimization_barrier(
        (own, root_after, root_before, root_far)
    )
    own = call(halves_kernel, (like((half, part // 2 * 3), BF16),) * 2, [own])

    before_top = shifted(own[0], 1)
    after_bottom = shifted(own[1], 3)
    before_bottom = shifted(own[1], 1)
    after_top = shifted(own[0], 3)
    far_top = shifted(before_top, 1)
    far_bottom = shifted(after_bottom, 3)

    def widened(value):
        return call(widen_kernel, like((half, 2 * part), BF16), [value])

    own = (widened(own[0]), widened(own[1]))
    before_top, before_bottom = widened(before_top), widened(before_bottom)
    after_top, after_bottom = widened(after_top), widened(after_bottom)
    root = root_right[0]
    own_square = call(square_kernel, like((8, 128)), [*own])
    stat = like((part, order))
    left, right = call(
        functools.partial(statistics_kernel, scale, (0,), True),
        (stat, stat),
        [place, *own, *own, left_stat[0], right_stat[0]],
        1,
        flops=2 * macs,
    )
    value = call(
        functools.partial(value_kernel, (0,), True),
        like((order, part)),
        [place, *own, root],
        1,
        flops=macs,
    )
    high, low = call(
        root_join_kernel,
        (like((order, order), BF16),) * 2,
        [place, root_left[0], root_after, root_before, root_far],
        1,
        cost=16 << 20,
    )
    near = (before_top, before_bottom, after_top, after_bottom)
    left, right = call(
        functools.partial(statistics_kernel, scale, (3, 1), False),
        (stat, stat),
        [place, *own, *near, left, right],
        1,
        flops=4 * macs,
    )
    value = call(
        functools.partial(value_kernel, (3, 1), False),
        like((order, part)),
        [place, *near, root, value],
        1,
        flops=2 * macs,
    )
    result, square, peak = call(
        functools.partial(result_kernel, 2),
        (like((order, part)), like((8, 128)), like((8, 128))),
        [place, far_top, far_bottom, root, value, high, low, own_square],
        1,
        flops=5 * macs,
    )
    squares = [square, shifted(square, 2), shifted(square, 1), shifted(square, 3)]
    codes = call(
        encode_kernel,
        like((owners, part * slab // 128, 128), BF16),
        [result, peak],
        cost=16 << 20,
    )
    codes = call(stamp_kernel, like((owners, part * slab // 128 + 8, 128), BF16), [peak, *squares, codes])
    returned = lax.all_to_all(codes, "fsdp", split_axis=0, concat_axis=0, tiled=True)
    left, right = call(
        functools.partial(statistics_kernel, scale, (2,), False),
        (stat, stat),
        [place, *own, widened(far_top), widened(far_bottom), left, right],
        1,
        flops=2 * macs,
    )
    direction = call(
        reorder_kernel, like((blocks, slab, part)), [block_owner, returned], 1
    )
    return (left[None], right[None], direction)


def solution(mesh):
    placed = (
        P("dp", None, "fsdp", None),
        P(),
        P("fsdp", "dp", None),
        P("fsdp", "dp", None),
        P("fsdp", "dp", None),
        P("fsdp", "dp", None),
    )
    return jax.shard_map(
        per_device,
        mesh=mesh,
        in_specs=placed,
        out_specs=(P("fsdp", "dp", None), P("fsdp", "dp", None), P(None, "fsdp", "dp")),
        check_vma=False,
    )
```

```python
import functools
import math

import jax
import jax.numpy as jnp
from jax import lax
from jax.experimental import pallas as pl
from jax.experimental.pallas import tpu as pltpu
from jax.sharding import PartitionSpec as P

AVERAGING = 0.9
GRAFT_EPS = 1e-06
VMEM_LIMIT = 24 * 1024 * 1024
STEPS = 1344
LARGEST = 252 * 128 + 127
FINE = 120.0

VMEM = pl.BlockSpec(memory_space=pltpu.VMEM)
SMEM = pl.BlockSpec(memory_space=pltpu.SMEM)
F32, BF16 = jnp.float32, jnp.bfloat16


def split(value):
    high = value.astype(BF16)
    low = (value - high.astype(F32)).astype(BF16)
    return high, low


def shrink(value):
    half = value.shape[1] // 2
    high = value.astype(BF16)
    wide = high.astype(F32)
    inverse = pl.reciprocal(jnp.where(wide == 0.0, 1.0, wide), approx=True)
    ratio = jnp.where(wide == 0.0, 0.0, (value - wide) * inverse)
    fine = jnp.clip(jnp.floor(ratio * (256.0 * FINE) + 0.5), -FINE, FINE)
    first, second = fine[:, :half], fine[:, half:]
    root = jnp.exp2(second * 0.5)
    word = (1.0 + jnp.abs(first) * (1.0 / 128.0)) * root * root
    return high, jnp.where(first < 0.0, -word, word).astype(BF16)


def widen(high, word):
    word = word.astype(F32)
    size = jnp.abs(word)
    second = jnp.floor(jnp.log(jnp.maximum(size, 1e-37)) * (1.0 / math.log(2.0)) + 0.01)
    root = jnp.exp2(second * -0.5)
    first = (size * root * root - 1.0) * 128.0
    first = jnp.where(word < 0.0, -first, first)
    fine = jnp.concatenate([first, second], axis=1) * (1.0 / (256.0 * FINE))
    return (high.astype(F32) * fine).astype(BF16)


def halves_kernel(whole_ref, top_ref, bottom_ref):
    half = top_ref.shape[0]
    top_ref[...] = whole_ref[:half, :]
    bottom_ref[...] = whole_ref[half:, :]


def widen_kernel(part_ref, out_ref):
    size = out_ref.shape[1] // 2
    high = part_ref[:, :size]
    out_ref[:, :size] = high
    out_ref[:, size:] = widen(high, part_ref[:, size:])


def dot3(left, right, left_dim, right_dim):
    dims = (((left_dim,), (right_dim,)), ((), ()))

    def one(a, b):
        return lax.dot_general(a, b, dims, preferred_element_type=F32)

    return one(left[0], right[0]) + (one(left[0], right[1]) + one(left[1], right[0]))


def like(shape, dtype=F32):
    return jax.ShapeDtypeStruct(shape, dtype)


def call(kernel, outs, operands, n_smem=0, smem_outs=(), flops=0, cost=4 << 20):
    several = isinstance(outs, tuple)
    out_specs = tuple(
        SMEM if i in smem_outs else VMEM for i in range(len(outs) if several else 1)
    )
    return pl.pallas_call(
        kernel,
        out_shape=outs,
        in_specs=[SMEM] * n_smem + [VMEM] * (len(operands) - n_smem),
        out_specs=out_specs if several else out_specs[0],
        compiler_params=pltpu.CompilerParams(vmem_limit_bytes=VMEM_LIMIT),
        cost_estimate=pl.CostEstimate(flops=flops, bytes_accessed=cost, transcendentals=0),
    )(*operands)


def around(index, size, parts):
    return pl.ds(pl.multiple_of(lax.rem(index, parts) * size, size), size)


def pack_kernel(place_ref, grad_ref, *out_refs):
    part = out_refs[0].shape[2]
    parts = len(out_refs)
    for k, out_ref in enumerate(out_refs):
        out_ref[...] = grad_ref[:, :, around(place_ref[0] + k, part, parts)]


def sum_kernel(owner_ref, *refs):
    *replica_refs, out_ref = refs
    part = replica_refs[0].shape[2]
    out_ref[...] = jnp.zeros_like(out_ref)

    @pl.loop(0, replica_refs[0].shape[0], unroll=8)
    def _(b):
        total = replica_refs[0][b].astype(F32)
        for ref in replica_refs[1:]:
            total = total + ref[b].astype(F32)
        owner = owner_ref[b]
        out_ref[owner, :, :part], out_ref[owner, :, part:] = shrink(total)


def root_pack_kernel(place_ref, root_ref, next_ref, previous_ref):
    size = root_ref.shape[0]
    parts = root_ref.shape[1] // size
    me = place_ref[0]

    def put(ref, slot, shift):
        high, word = shrink(root_ref[:, around(me + shift, size, parts)])
        ref[slot, :, :size] = high
        ref[slot, :, size:] = word

    for slot in range(3):
        put(next_ref, slot, slot)
    put(previous_ref, 0, 0)
    put(previous_ref, 1, parts - 1)


def root_join_kernel(place_ref, root_ref, after_ref, before_ref, far_ref, high_ref, low_ref):
    size = root_ref.shape[0]
    parts = root_ref.shape[1] // size
    me = place_ref[0]

    def put(i, j, value):
        rows, columns = around(me + i, size, parts), around(me + j, size, parts)
        for ref, half in zip((high_ref, low_ref), value):
            ref[rows, columns] = half
            if i != j:
                ref[columns, rows] = half.astype(F32).T.astype(BF16)

    def block(ref, slot):
        high = ref[slot, :, :size]
        return high, widen(high, ref[slot, :, size:])

    for j in range(parts):
        put(0, j, split(root_ref[:, around(me + j, size, parts)]))
    put(1, 1, block(after_ref, 0))
    put(1, 2, block(after_ref, 1))
    put(1, 3, block(after_ref, 2))
    put(3, 3, block(before_ref, 0))
    put(3, 2, block(before_ref, 1))
    put(2, 2, block(far_ref, 0))


def own_half(refs, me, part):
    rows = pl.ds(pl.multiple_of(lax.rem(me, 2) * part, part), part)
    top, bottom = refs[0][rows, :], refs[1][rows, :]
    return jnp.where(me < 2, top, bottom)


def pair(value):
    part = value.shape[1] // 2
    return value[:, :part], value[:, part:]


def statistics_kernel(scale, shifts, first, place_ref, *refs):
    count = 2 * len(shifts)
    own, parts = refs[:2], refs[2 : 2 + count]
    left_in, right_in, left_out, right_out = refs[2 + count :]
    me = place_ref[0]
    part, order = left_in.shape
    half = order // 2
    keep = AVERAGING if first else 1.0
    right_out[...] = right_in[...] * keep
    left = left_in[...] * keep
    sums = [left[:, :half], left[:, half:]]
    for i, shift in enumerate(shifts):
        blocks = parts[2 * i : 2 * i + 2]
        mine = pair(own_half(blocks, me, part))
        halves = [pair(ref[...]) for ref in blocks]
        for h in range(2):
            sums[h] = sums[h] + scale * dot3(mine, halves[h], 1, 1)
        term = dot3(pair(own[0][...]), halves[0], 0, 0) + dot3(pair(own[1][...]), halves[1], 0, 0)
        columns = around(me + shift, part, order // part)
        right_out[:, columns] += scale * term
    left_out[:, :half] = sums[0]
    left_out[:, half:] = sums[1]


def value_terms(me, shifts, parts, root_ref):
    part, order = root_ref.shape
    sums = [None, None]
    for i, shift in enumerate(shifts):
        root = split(root_ref[:, around(me + shift, part, order // part)])
        for h in range(2):
            term = dot3(parts[2 * i + h], root, 1, 1)
            sums[h] = term if sums[h] is None else sums[h] + term
    return sums


def value_kernel(shifts, first, place_ref, *refs):
    count = 2 * len(shifts)
    parts, root_ref = refs[:count], refs[count]
    *value_in, value_out = refs[count + 1 :]
    half = value_out.shape[0] // 2
    sums = value_terms(place_ref[0], shifts, [pair(ref[...]) for ref in parts], root_ref)
    for h in range(2):
        rows = slice(h * half, (h + 1) * half)
        value_out[rows, :] = sums[h] if first else sums[h] + value_in[0][rows, :]


def square_kernel(top_ref, bottom_ref, out_ref):
    total = jnp.zeros((), F32)
    for ref in (top_ref, bottom_ref):
        high, low = pair(ref[...])
        whole = high.astype(F32) + low.astype(F32)
        total = total + jnp.sum(whole * whole)
    out_ref[...] = jnp.full(out_ref.shape, total)


def result_kernel(
    shift, place_ref, top_ref, bottom_ref, root_ref, value_ref, high_ref, low_ref, own_square, out_ref, square_ref, peak_ref
):
    order, part = value_ref.shape
    half = order // 2
    coded = [(ref[:, :part], ref[:, part:]) for ref in (top_ref, bottom_ref)]
    pieces = [(high, widen(high, word)) for high, word in coded]
    sums = value_terms(place_ref[0], (shift,), pieces, root_ref)
    halves = [split(sums[h] + value_ref[h * half : (h + 1) * half, :]) for h in range(2)]
    value = [jnp.concatenate([halves[0][i], halves[1][i]], axis=0) for i in range(2)]
    total = jnp.zeros((), F32)
    peak = jnp.zeros((), F32)
    for i in range(2):
        rows = slice(i * half, (i + 1) * half)
        block = dot3((high_ref[rows, :], low_ref[rows, :]), value, 1, 0)
        out_ref[rows, :] = block
        total = total + jnp.sum(block * block)
        peak = jnp.maximum(peak, jnp.max(jnp.abs(block)))
    first = lax.broadcasted_iota(jnp.int32, square_ref.shape, 1) == 0
    square_ref[...] = jnp.where(first, own_square[...], total)
    peak_ref[...] = jnp.full(peak_ref.shape, peak)


def encode(ratio):
    size = jnp.abs(ratio)
    code = jnp.floor(jnp.log(jnp.maximum(size, 1e-30)) * (STEPS / math.log(2.0)) + (LARGEST + 0.5))
    code = jnp.minimum(code, float(LARGEST))
    exponent = jnp.floor(code * (1.0 / 128.0))
    root = jnp.exp2((exponent - 126.0) * 0.5)
    number = (1.0 + (code - exponent * 128.0) * (1.0 / 128.0)) * root * root
    number = jnp.where(code < 128.0, 0.0, number)
    return jnp.where(ratio < 0.0, -number, number).astype(BF16)


def decode(number):
    size = jnp.abs(number)
    exponent = jnp.floor(jnp.log(jnp.maximum(size, 2e-38)) * (1.0 / math.log(2.0)) + 0.002)
    root = jnp.exp2(exponent * -0.5)
    code = 128.0 * (exponent + 125.0 + size * root * root)
    value = jnp.exp2((code - LARGEST) * (1.0 / STEPS))
    value = jnp.where(size == 0.0, 0.0, value)
    return jnp.where(number < 0.0, -value, value)


def encode_kernel(value_ref, peak_ref, out_ref):
    slab = value_ref.shape[0] // out_ref.shape[0]
    lanes = out_ref.shape[2]
    peak = jnp.max(peak_ref[...])
    inverse = jnp.where(peak > 1e-37, 1.0 / jnp.maximum(peak, 1e-37), 0.0)
    pieces = value_ref.shape[1] // lanes

    @pl.loop(0, out_ref.shape[0], unroll=16)
    def _(o):
        rows = pl.ds(pl.multiple_of(o * slab, slab), slab)
        for i in range(pieces):
            value = value_ref[rows, i * lanes : (i + 1) * lanes]
            out_ref[o, i * slab : (i + 1) * slab, :] = encode(value * inverse)


def stamp_kernel(peak_ref, *refs):
    *square_refs, codes_ref, out_ref = refs
    total = square_refs[0][...]
    for ref in square_refs[1:]:
        total = total + ref[...]
    gradient, result = total[:, :1], total[:, 1:2]
    scale = peak_ref[...] * (jnp.sqrt(gradient) * lax.rsqrt(result + GRAFT_EPS))
    row = lax.broadcasted_iota(jnp.int32, scale.shape, 0)
    high = scale.astype(BF16).astype(F32)
    middle = (scale - high).astype(BF16).astype(F32)
    low = scale - high - middle
    value = jnp.where(row == 0, high, jnp.where(row == 1, middle, jnp.where(row == 2, low, 0.0)))

    @pl.loop(0, out_ref.shape[0], unroll=8)
    def _(o):
        packet = jnp.concatenate([codes_ref[o].astype(F32), value], axis=0)
        out_ref[o] = packet.astype(BF16)


def reorder_kernel(owner_ref, returned_ref, out_ref):
    slab = out_ref.shape[1]
    lanes = returned_ref.shape[2]
    pieces = out_ref.shape[2] // lanes

    @pl.loop(0, out_ref.shape[0], unroll=16)
    def _(b):
        packet = returned_ref[owner_ref[b]].astype(F32)
        scale = jnp.sum(packet[pieces * slab :], axis=0, keepdims=True)
        for i in range(pieces):
            value = decode(packet[i * slab : (i + 1) * slab])
            out_ref[b, :, i * lanes : (i + 1) * lanes] = value * scale


def per_device(grad_parts, block_owner, left_stat, right_stat, root_left, root_right):
    owners = lax.axis_size("fsdp")
    replicas = lax.axis_size("dp")
    me = lax.axis_index("dp")
    part, order = root_left.shape[1:]
    blocks, slab = grad_parts.shape[1:3]
    scale = (1.0 - AVERAGING) / order
    place = me.astype(jnp.int32).reshape(1)
    half = order // 2
    macs = 2 * 3 * part * part * order

    def shifted(value, k):
        return lax.ppermute(value, "dp", [(i, (i + k) % replicas) for i in range(replicas)])

    packed = call(
        pack_kernel,
        (like((blocks, slab, part), BF16),) * replicas,
        [place, grad_parts[0]],
        1,
    )
    arrived = [packed[0]] + [shifted(packed[k], k) for k in (2, 1, 3)]
    to_previous, to_next = call(
        root_pack_kernel,
        tuple(like((n, part, part // 2 * 3), BF16) for n in (3, 2)),
        [place, root_left[0]],
        1,
    )
    arrived, to_previous, to_next = lax.optimization_barrier((arrived, to_previous, to_next))
    root_after = shifted(to_previous, 3)
    root_before = shifted(to_next, 1)
    root_far = shifted(root_before[:1], 1)
    outgoing = call(
        sum_kernel, like((owners, slab, part // 2 * 3), BF16), [block_owner, *arrived], 1
    )
    own = lax.all_to_all(outgoing, "fsdp", split_axis=0, concat_axis=0, tiled=True)
    own = own.reshape(order, part // 2 * 3)
    own, root_after, root_before, root_far = lax.optimization_barrier(
        (own, root_after, root_before, root_far)
    )
    own = call(halves_kernel, (like((half, part // 2 * 3), BF16),) * 2, [own])

    before_top = shifted(own[0], 1)
    after_bottom = shifted(own[1], 3)
    before_bottom = shifted(own[1], 1)
    after_top = shifted(own[0], 3)
    far_top = shifted(before_top, 1)
    far_bottom = shifted(after_bottom, 3)

    def widened(value):
        return call(widen_kernel, like((half, 2 * part), BF16), [value])

    own = (widened(own[0]), widened(own[1]))
    before_top, before_bottom = widened(before_top), widened(before_bottom)
    after_top, after_bottom = widened(after_top), widened(after_bottom)
    root = root_right[0]
    own_square = call(square_kernel, like((8, 128)), [*own])
    stat = like((part, order))
    left, right = call(
        functools.partial(statistics_kernel, scale, (0,), True),
        (stat, stat),
        [place, *own, *own, left_stat[0], right_stat[0]],
        1,
        flops=2 * macs,
    )
    value = call(
        functools.partial(value_kernel, (0,), True),
        like((order, part)),
        [place, *own, root],
        1,
        flops=macs,
    )
    high, low = call(
        root_join_kernel,
        (like((order, order), BF16),) * 2,
        [place, root_left[0], root_after, root_before, root_far],
        1,
        cost=16 << 20,
    )
    near = (before_top, before_bottom, after_top, after_bottom)
    left, right = call(
        functools.partial(statistics_kernel, scale, (3, 1), False),
        (stat, stat),
        [place, *own, *near, left, right],
        1,
        flops=4 * macs,
    )
    value = call(
        functools.partial(value_kernel, (3, 1), False),
        like((order, part)),
        [place, *near, root, value],
        1,
        flops=2 * macs,
    )
    result, square, peak = call(
        functools.partial(result_kernel, 2),
        (like((order, part)), like((8, 128)), like((8, 128))),
        [place, far_top, far_bottom, root, value, high, low, own_square],
        1,
        flops=5 * macs,
    )
    squares = [square, shifted(square, 2), shifted(square, 1), shifted(square, 3)]
    codes = call(
        encode_kernel,
        like((owners, part * slab // 128, 128), BF16),
        [result, peak],
        cost=16 << 20,
    )
    codes = call(stamp_kernel, like((owners, part * slab // 128 + 8, 128), BF16), [peak, *squares, codes])
    returned = lax.all_to_all(codes, "fsdp", split_axis=0, concat_axis=0, tiled=True)
    left, right = call(
        functools.partial(statistics_kernel, scale, (2,), False),
        (stat, stat),
        [place, *own, widened(far_top), widened(far_bottom), left, right],
        1,
        flops=2 * macs,
    )
    direction = call(
        reorder_kernel, like((blocks, slab, part)), [block_owner, returned], 1
    )
    return (left[None], right[None], direction)


def solution(mesh):
    placed = (
        P("dp", None, "fsdp", None),
        P(),
        P("fsdp", "dp", None),
        P("fsdp", "dp", None),
        P("fsdp", "dp", None),
        P("fsdp", "dp", None),
    )
    return jax.shard_map(
        per_device,
        mesh=mesh,
        in_specs=placed,
        out_specs=(P("fsdp", "dp", None), P("fsdp", "dp", None), P(None, "fsdp", "dp")),
        check_vma=False,
    )
```

```python
import functools
import math

import jax
import jax.numpy as jnp
from jax import lax
from jax.experimental import pallas as pl
from jax.experimental.pallas import tpu as pltpu
from jax.sharding import PartitionSpec as P

AVERAGING = 0.9
GRAFT_EPS = 1e-06
VMEM_LIMIT = 24 * 1024 * 1024
STEPS = 1344
LARGEST = 252 * 128 + 127
FINE = 120.0

VMEM = pl.BlockSpec(memory_space=pltpu.VMEM)
SMEM = pl.BlockSpec(memory_space=pltpu.SMEM)
F32, BF16 = jnp.float32, jnp.bfloat16


def split(value):
    high = value.astype(BF16)
    low = (value - high.astype(F32)).astype(BF16)
    return high, low


def shrink(value):
    half = value.shape[1] // 2
    high = value.astype(BF16)
    wide = high.astype(F32)
    inverse = pl.reciprocal(jnp.where(wide == 0.0, 1.0, wide), approx=True)
    ratio = jnp.where(wide == 0.0, 0.0, (value - wide) * inverse)
    fine = jnp.clip(jnp.floor(ratio * (256.0 * FINE) + 0.5), -FINE, FINE)
    first, second = fine[:, :half], fine[:, half:]
    root = jnp.exp2(second * 0.5)
    word = (1.0 + jnp.abs(first) * (1.0 / 128.0)) * root * root
    return high, jnp.where(first < 0.0, -word, word).astype(BF16)


def widen(high, word):
    word = word.astype(F32)
    size = jnp.abs(word)
    second = jnp.floor(jnp.log(jnp.maximum(size, 1e-37)) * (1.0 / math.log(2.0)) + 0.01)
    root = jnp.exp2(second * -0.5)
    first = (size * root * root - 1.0) * 128.0
    first = jnp.where(word < 0.0, -first, first)
    fine = jnp.concatenate([first, second], axis=1) * (1.0 / (256.0 * FINE))
    return (high.astype(F32) * fine).astype(BF16)


def halves_kernel(whole_ref, top_ref, bottom_ref):
    half = top_ref.shape[0]
    top_ref[...] = whole_ref[:half, :]
    bottom_ref[...] = whole_ref[half:, :]


def widen_kernel(part_ref, out_ref):
    size = out_ref.shape[1] // 2
    high = part_ref[:, :size]
    out_ref[:, :size] = high
    out_ref[:, size:] = widen(high, part_ref[:, size:])


def dot3(left, right, left_dim, right_dim):
    dims = (((left_dim,), (right_dim,)), ((), ()))

    def one(a, b):
        return lax.dot_general(a, b, dims, preferred_element_type=F32)

    return one(left[0], right[0]) + (one(left[0], right[1]) + one(left[1], right[0]))


def like(shape, dtype=F32):
    return jax.ShapeDtypeStruct(shape, dtype)


def call(kernel, outs, operands, n_smem=0, smem_outs=(), flops=0, cost=4 << 20, staged=False):
    several = isinstance(outs, tuple)
    out_specs = tuple(
        SMEM if i in smem_outs else VMEM for i in range(len(outs) if several else 1)
    )
    scratch = []
    if staged:
        out_specs = (pl.BlockSpec(memory_space=pl.ANY),)
        parts = math.gcd(outs.shape[0], 4)
        scratch = [pltpu.VMEM(outs.shape, outs.dtype), pltpu.SemaphoreType.DMA((parts,))]
    return pl.pallas_call(
        kernel,
        out_shape=outs,
        in_specs=[SMEM] * n_smem + [VMEM] * (len(operands) - n_smem),
        out_specs=out_specs if several else out_specs[0],
        scratch_shapes=scratch,
        compiler_params=pltpu.CompilerParams(vmem_limit_bytes=VMEM_LIMIT),
        cost_estimate=pl.CostEstimate(flops=flops, bytes_accessed=cost, transcendentals=0),
    )(*operands)


def around(index, size, parts):
    return pl.ds(pl.multiple_of(lax.rem(index, parts) * size, size), size)


def pack_kernel(place_ref, grad_ref, *out_refs):
    part = out_refs[0].shape[2]
    parts = len(out_refs)
    for k, out_ref in enumerate(out_refs):
        out_ref[...] = grad_ref[:, :, around(place_ref[0] + k, part, parts)]


def sum_kernel(owner_ref, *refs):
    *replica_refs, out_ref = refs
    part = replica_refs[0].shape[2]
    out_ref[...] = jnp.zeros_like(out_ref)

    @pl.loop(0, replica_refs[0].shape[0], unroll=8)
    def _(b):
        total = replica_refs[0][b].astype(F32)
        for ref in replica_refs[1:]:
            total = total + ref[b].astype(F32)
        owner = owner_ref[b]
        out_ref[owner, :, :part], out_ref[owner, :, part:] = shrink(total)


def root_pack_kernel(place_ref, root_ref, next_ref, previous_ref):
    size = root_ref.shape[0]
    parts = root_ref.shape[1] // size
    me = place_ref[0]

    def put(ref, slot, shift):
        high, word = shrink(root_ref[:, around(me + shift, size, parts)])
        ref[slot, :, :size] = high
        ref[slot, :, size:] = word

    for slot in range(3):
        put(next_ref, slot, slot)
    put(previous_ref, 0, 0)
    put(previous_ref, 1, parts - 1)


def root_join_kernel(place_ref, root_ref, after_ref, before_ref, far_ref, high_ref, low_ref):
    size = root_ref.shape[0]
    parts = root_ref.shape[1] // size
    me = place_ref[0]

    def put(i, j, value):
        rows, columns = around(me + i, size, parts), around(me + j, size, parts)
        for ref, half in zip((high_ref, low_ref), value):
            ref[rows, columns] = half
            if i != j:
                ref[columns, rows] = half.astype(F32).T.astype(BF16)

    def block(ref, slot):
        high = ref[slot, :, :size]
        return high, widen(high, ref[slot, :, size:])

    for j in range(parts):
        put(0, j, split(root_ref[:, around(me + j, size, parts)]))
    put(1, 1, block(after_ref, 0))
    put(1, 2, block(after_ref, 1))
    put(1, 3, block(after_ref, 2))
    put(3, 3, block(before_ref, 0))
    put(3, 2, block(before_ref, 1))
    put(2, 2, block(far_ref, 0))


def own_half(refs, me, part):
    rows = pl.ds(pl.multiple_of(lax.rem(me, 2) * part, part), part)
    top, bottom = refs[0][rows, :], refs[1][rows, :]
    return jnp.where(me < 2, top, bottom)


def pair(value):
    part = value.shape[1] // 2
    return value[:, :part], value[:, part:]


def statistics_kernel(scale, shifts, first, place_ref, *refs):
    count = 2 * len(shifts)
    own, parts = refs[:2], refs[2 : 2 + count]
    left_in, right_in, left_out, right_out = refs[2 + count :]
    me = place_ref[0]
    part, order = left_in.shape
    half = order // 2
    keep = AVERAGING if first else 1.0
    right_out[...] = right_in[...] * keep
    left = left_in[...] * keep
    sums = [left[:, :half], left[:, half:]]
    for i, shift in enumerate(shifts):
        blocks = parts[2 * i : 2 * i + 2]
        mine = pair(own_half(blocks, me, part))
        halves = [pair(ref[...]) for ref in blocks]
        for h in range(2):
            sums[h] = sums[h] + scale * dot3(mine, halves[h], 1, 1)
        term = dot3(pair(own[0][...]), halves[0], 0, 0) + dot3(pair(own[1][...]), halves[1], 0, 0)
        columns = around(me + shift, part, order // part)
        right_out[:, columns] += scale * term
    left_out[:, :half] = sums[0]
    left_out[:, half:] = sums[1]


def value_terms(me, shifts, parts, root_ref):
    part, order = root_ref.shape
    sums = [None, None]
    for i, shift in enumerate(shifts):
        root = split(root_ref[:, around(me + shift, part, order // part)])
        for h in range(2):
            term = dot3(parts[2 * i + h], root, 1, 1)
            sums[h] = term if sums[h] is None else sums[h] + term
    return sums


def value_kernel(shifts, first, place_ref, *refs):
    count = 2 * len(shifts)
    parts, root_ref = refs[:count], refs[count]
    *value_in, value_out = refs[count + 1 :]
    half = value_out.shape[0] // 2
    sums = value_terms(place_ref[0], shifts, [pair(ref[...]) for ref in parts], root_ref)
    for h in range(2):
        rows = slice(h * half, (h + 1) * half)
        value_out[rows, :] = sums[h] if first else sums[h] + value_in[0][rows, :]


def square_kernel(top_ref, bottom_ref, out_ref):
    total = jnp.zeros((), F32)
    for ref in (top_ref, bottom_ref):
        high, low = pair(ref[...])
        whole = high.astype(F32) + low.astype(F32)
        total = total + jnp.sum(whole * whole)
    out_ref[...] = jnp.full(out_ref.shape, total)


def result_kernel(
    shift, place_ref, top_ref, bottom_ref, root_ref, value_ref, high_ref, low_ref, own_square, out_ref, square_ref, peak_ref
):
    order, part = value_ref.shape
    half = order // 2
    coded = [(ref[:, :part], ref[:, part:]) for ref in (top_ref, bottom_ref)]
    pieces = [(high, widen(high, word)) for high, word in coded]
    sums = value_terms(place_ref[0], (shift,), pieces, root_ref)
    halves = [split(sums[h] + value_ref[h * half : (h + 1) * half, :]) for h in range(2)]
    value = [jnp.concatenate([halves[0][i], halves[1][i]], axis=0) for i in range(2)]
    total = jnp.zeros((), F32)
    peak = jnp.zeros((), F32)
    for i in range(2):
        rows = slice(i * half, (i + 1) * half)
        block = dot3((high_ref[rows, :], low_ref[rows, :]), value, 1, 0)
        out_ref[rows, :] = block
        total = total + jnp.sum(block * block)
        peak = jnp.maximum(peak, jnp.max(jnp.abs(block)))
    first = lax.broadcasted_iota(jnp.int32, square_ref.shape, 1) == 0
    square_ref[...] = jnp.where(first, own_square[...], total)
    peak_ref[...] = jnp.full(peak_ref.shape, peak)


def encode(ratio):
    size = jnp.abs(ratio)
    code = jnp.floor(jnp.log(jnp.maximum(size, 1e-30)) * (STEPS / math.log(2.0)) + (LARGEST + 0.5))
    code = jnp.minimum(code, float(LARGEST))
    exponent = jnp.floor(code * (1.0 / 128.0))
    root = jnp.exp2((exponent - 126.0) * 0.5)
    number = (1.0 + (code - exponent * 128.0) * (1.0 / 128.0)) * root * root
    number = jnp.where(code < 128.0, 0.0, number)
    return jnp.where(ratio < 0.0, -number, number).astype(BF16)


def decode(number):
    size = jnp.abs(number)
    exponent = jnp.floor(jnp.log(jnp.maximum(size, 2e-38)) * (1.0 / math.log(2.0)) + 0.002)
    root = jnp.exp2(exponent * -0.5)
    code = 128.0 * (exponent + 125.0 + size * root * root)
    value = jnp.exp2((code - LARGEST) * (1.0 / STEPS))
    value = jnp.where(size == 0.0, 0.0, value)
    return jnp.where(number < 0.0, -value, value)


def encode_kernel(value_ref, peak_ref, out_ref):
    slab = value_ref.shape[0] // out_ref.shape[0]
    lanes = out_ref.shape[2]
    peak = jnp.max(peak_ref[...])
    inverse = jnp.where(peak > 1e-37, 1.0 / jnp.maximum(peak, 1e-37), 0.0)
    pieces = value_ref.shape[1] // lanes

    @pl.loop(0, out_ref.shape[0], unroll=16)
    def _(o):
        rows = pl.ds(pl.multiple_of(o * slab, slab), slab)
        for i in range(pieces):
            value = value_ref[rows, i * lanes : (i + 1) * lanes]
            out_ref[o, i * slab : (i + 1) * slab, :] = encode(value * inverse)


def in_parts(fill, stage_ref, out_ref, semaphores):
    parts = semaphores.shape[0]
    size = stage_ref.shape[0] // parts
    copies = []
    for p in range(parts):
        pl.loop(p * size, (p + 1) * size, unroll=size)(fill)
        rows = pl.ds(p * size, size)
        copy = pltpu.make_async_copy(stage_ref.at[rows], out_ref.at[rows], semaphores.at[p])
        copy.start()
        copies.append(copy)
    for copy in copies:
        copy.wait()


def stamp_kernel(peak_ref, *refs):
    *square_refs, codes_ref, out_ref, stage_ref, semaphores = refs
    total = square_refs[0][...]
    for ref in square_refs[1:]:
        total = total + ref[...]
    gradient, result = total[:, :1], total[:, 1:2]
    scale = peak_ref[...] * (jnp.sqrt(gradient) * lax.rsqrt(result + GRAFT_EPS))
    row = lax.broadcasted_iota(jnp.int32, scale.shape, 0)
    high = scale.astype(BF16).astype(F32)
    middle = (scale - high).astype(BF16).astype(F32)
    low = scale - high - middle
    value = jnp.where(row == 0, high, jnp.where(row == 1, middle, jnp.where(row == 2, low, 0.0)))

    def fill(o):
        packet = jnp.concatenate([codes_ref[o].astype(F32), value], axis=0)
        stage_ref[o] = packet.astype(BF16)

    in_parts(fill, stage_ref, out_ref, semaphores)


def reorder_kernel(owner_ref, returned_ref, out_ref, stage_ref, semaphores):
    slab = out_ref.shape[1]
    lanes = returned_ref.shape[2]
    pieces = out_ref.shape[2] // lanes

    def fill(b):
        packet = returned_ref[owner_ref[b]].astype(F32)
        scale = jnp.sum(packet[pieces * slab :], axis=0, keepdims=True)
        for i in range(pieces):
            value = decode(packet[i * slab : (i + 1) * slab])
            stage_ref[b, :, i * lanes : (i + 1) * lanes] = value * scale

    in_parts(fill, stage_ref, out_ref, semaphores)


def per_device(grad_parts, block_owner, left_stat, right_stat, root_left, root_right):
    owners = lax.axis_size("fsdp")
    replicas = lax.axis_size("dp")
    me = lax.axis_index("dp")
    part, order = root_left.shape[1:]
    blocks, slab = grad_parts.shape[1:3]
    scale = (1.0 - AVERAGING) / order
    place = me.astype(jnp.int32).reshape(1)
    half = order // 2
    macs = 2 * 3 * part * part * order

    def shifted(value, k):
        return lax.ppermute(value, "dp", [(i, (i + k) % replicas) for i in range(replicas)])

    packed = call(
        pack_kernel,
        (like((blocks, slab, part), BF16),) * replicas,
        [place, grad_parts[0]],
        1,
    )
    arrived = [packed[0]] + [shifted(packed[k], k) for k in (2, 1, 3)]
    to_previous, to_next = call(
        root_pack_kernel,
        tuple(like((n, part, part // 2 * 3), BF16) for n in (3, 2)),
        [place, root_left[0]],
        1,
    )
    arrived, to_previous, to_next = lax.optimization_barrier((arrived, to_previous, to_next))
    root_after = shifted(to_previous, 3)
    root_before = shifted(to_next, 1)
    root_far = shifted(root_before[:1], 1)
    outgoing = call(
        sum_kernel, like((owners, slab, part // 2 * 3), BF16), [block_owner, *arrived], 1
    )
    own = lax.all_to_all(outgoing, "fsdp", split_axis=0, concat_axis=0, tiled=True)
    own = own.reshape(order, part // 2 * 3)
    own, root_after, root_before, root_far = lax.optimization_barrier(
        (own, root_after, root_before, root_far)
    )
    own = call(halves_kernel, (like((half, part // 2 * 3), BF16),) * 2, [own])

    before_top = shifted(own[0], 1)
    after_bottom = shifted(own[1], 3)
    before_bottom = shifted(own[1], 1)
    after_top = shifted(own[0], 3)
    far_top = shifted(before_top, 1)
    far_bottom = shifted(after_bottom, 3)

    def widened(value):
        return call(widen_kernel, like((half, 2 * part), BF16), [value])

    own = (widened(own[0]), widened(own[1]))
    before_top, before_bottom = widened(before_top), widened(before_bottom)
    after_top, after_bottom = widened(after_top), widened(after_bottom)
    root = root_right[0]
    own_square = call(square_kernel, like((8, 128)), [*own])
    stat = like((part, order))
    left, right = call(
        functools.partial(statistics_kernel, scale, (0,), True),
        (stat, stat),
        [place, *own, *own, left_stat[0], right_stat[0]],
        1,
        flops=2 * macs,
    )
    value = call(
        functools.partial(value_kernel, (0,), True),
        like((order, part)),
        [place, *own, root],
        1,
        flops=macs,
    )
    high, low = call(
        root_join_kernel,
        (like((order, order), BF16),) * 2,
        [place, root_left[0], root_after, root_before, root_far],
        1,
        cost=16 << 20,
    )
    near = (before_top, before_bottom, after_top, after_bottom)
    left, right = call(
        functools.partial(statistics_kernel, scale, (3, 1), False),
        (stat, stat),
        [place, *own, *near, left, right],
        1,
        flops=4 * macs,
    )
    value = call(
        functools.partial(value_kernel, (3, 1), False),
        like((order, part)),
        [place, *near, root, value],
        1,
        flops=2 * macs,
    )
    result, square, peak = call(
        functools.partial(result_kernel, 2),
        (like((order, part)), like((8, 128)), like((8, 128))),
        [place, far_top, far_bottom, root, value, high, low, own_square],
        1,
        flops=5 * macs,
    )
    squares = [square, shifted(square, 2), shifted(square, 1), shifted(square, 3)]
    codes = call(
        encode_kernel,
        like((owners, part * slab // 128, 128), BF16),
        [result, peak],
        cost=16 << 20,
    )
    codes = call(stamp_kernel, like((owners, part * slab // 128 + 8, 128), BF16), [peak, *squares, codes], staged=True)
    returned = lax.all_to_all(codes, "fsdp", split_axis=0, concat_axis=0, tiled=True)
    left, right = call(
        functools.partial(statistics_kernel, scale, (2,), False),
        (stat, stat),
        [place, *own, widened(far_top), widened(far_bottom), left, right],
        1,
        flops=2 * macs,
    )
    direction = call(
        reorder_kernel, like((blocks, slab, part)), [block_owner, returned], 1, staged=True
    )
    return (left[None], right[None], direction)


def solution(mesh):
    placed = (
        P("dp", None, "fsdp", None),
        P(),
        P("fsdp", "dp", None),
        P("fsdp", "dp", None),
        P("fsdp", "dp", None),
        P("fsdp", "dp", None),
    )
    return jax.shard_map(
        per_device,
        mesh=mesh,
        in_specs=placed,
        out_specs=(P("fsdp", "dp", None), P("fsdp", "dp", None), P(None, "fsdp", "dp")),
        check_vma=False,
    )
```
